32 devices in a mesh: board: 8 (over y, x, core), hand: 4 (over z).
Axes of the slice: x: 2, y: 2, z: 4, core: 2. Of those that a mesh axis runs over, the one named last changes fastest.
Arguments:
- reach_pre: float32 [1408], P(('board', 'hand')), may hold values from 0.05 to 1
- strategy: bfloat16 [64, 128, 1408], P('board', None, 'hand'), may hold values from 0 to 1
- ranks: int32 [64, 8, 1408], P('board'), may hold values from 0 to 94
- boards: int32 [64, 8, 5], P('board'), may hold values from 0 to 51, as said below
- river_live: int32 [64], P('board'), may hold values from 1 to 8, as said below
- iso_weight: int32 [64], P('board'), may hold values from 1 to 24
- pot: float32 [128], replicated, may hold values from 2 to 24
- line_act: int32 [128], replicated, may hold values from 0 to 2
Outputs:
- preflop_value: float32 [1408], P('hand')
The draws below stay inside these ranges and needn't reach their ends.
Inputs may be any that keep to these rules, and one draw needn't show every extreme that they name: `boards`: the five cards of a runout are distinct; all runouts of a flop share their first three cards. `river_live`: in every draw some flop has all 8 runouts live.
All inputs are finite; a program needn't handle non-finite values.
Results may differ from the reference program's by a relative error of at most 0.0003.
Values may be sent and summed in bfloat16 or wider, within the bound.
No kernel may reach another device: no remote copies, remote signals or barrier semaphores. Data moves between devices by JAX's collectives and lax.ppermute only.
A program may use at most 64 MiB of HBM per device.

```python
import math
import jax
import jax.numpy as jnp
import numpy as np
from jax import lax

HANDS = 1326
HPAD = 1408
RIV = 8
LINES = 128
ACTS = 3
FLOPS = 64


def draw_ranks(key, part):
    base_rank = jax.random.randint(jax.random.fold_in(key, 11), (1, 1, HPAD), 0, 32)
    noise_rank = jax.random.randint(jax.random.fold_in(key, 12), (FLOPS, RIV, HPAD), 0, 64)
    drawn = (base_rank + noise_rank).astype(jnp.int32)
    entries = FLOPS * RIV * HPAD
    position = jnp.arange(entries, dtype=jnp.int32).reshape(FLOPS, RIV, HPAD)
    low_at = jax.random.randint(jax.random.fold_in(key, 13), (), 0, entries)
    high_at = (low_at + 1 + jax.random.randint(jax.random.fold_in(key, 14), (), 0, entries - 1)) % entries
    drawn = jnp.where(position == low_at, 0, drawn)
    drawn = jnp.where(position == high_at, 94, drawn)
    return drawn.astype(jnp.int32)


def draw_boards(key, part):
    scores = jax.random.randint(jax.random.fold_in(key, 21), (FLOPS, 52), 0, 1 << 20) * 64 + jnp.arange(52, dtype=jnp.int32)[None, :]
    order = jnp.argsort(scores, axis=1).astype(jnp.int32)
    flop_cards = jnp.broadcast_to(order[:, None, 0:3], (FLOPS, RIV, 3))
    turn_cards = order[:, 3:3 + 2 * RIV:2]
    river_cards = order[:, 4:4 + 2 * RIV:2]
    return jnp.concatenate([flop_cards, turn_cards[:, :, None], river_cards[:, :, None]], axis=2).astype(jnp.int32)


def draw_river_live(key, part):
    heavy = jax.random.randint(jax.random.fold_in(key, 31), (FLOPS,), 0, 3) == 0
    counts = jax.random.randint(jax.random.fold_in(key, 32), (FLOPS,), 1, RIV + 1)
    counts = jnp.where(heavy, counts, 1)
    chosen = jax.random.randint(jax.random.fold_in(key, 33), (), 0, FLOPS)
    return jnp.where(jnp.arange(FLOPS, dtype=jnp.int32) == chosen, RIV, counts).astype(jnp.int32)


def set_ends(values, rng, smallest, high):
    dims = values.shape
    place = [jax.random.randint(jax.random.fold_in(rng, axis), (), 0, dims[axis]) for axis in range(len(dims))]
    values = values.at[tuple(place)].set(smallest)
    longest = dims.index(max(dims))
    place[longest] = (place[longest] + 1) % dims[longest]
    return values.at[tuple(place)].set(high)


def steps_of(stream_key, shape, shards, least, top_value):
    gain, own = 1.0, jax.random.fold_in(stream_key, 6)
    for dim, parts in shards:
        steps = jnp.exp(jax.random.uniform(jax.random.fold_in(own, dim), (parts,), jnp.float32, least / len(shards), top_value / len(shards)))
        gain = gain * jnp.repeat(steps, shape[dim] // parts).reshape([-1 if axis == dim else 1 for axis in range(len(shape))])
    return gain


def setup_inputs(seed: int = 0) -> dict:
    seeds = jax.random.split(jax.random.key(seed), 9)
    reach_pre = jnp.clip(jnp.exp(math.log(1.0) - 2.9957323 * jax.random.uniform(seeds[0], (HPAD,), jnp.float32) ** steps_of(seeds[0], (HPAD,), ((0, 32),), -0.2, 0.2)), 0.05, 1.0)
    strategy = jnp.clip(1.0 * jax.random.uniform(seeds[1], (FLOPS, LINES, HPAD), jnp.float32) ** steps_of(seeds[1], (FLOPS, LINES, HPAD), ((0, 8), (2, 4)), -0.2, 0.2), 0.0, 1.0).astype(jnp.bfloat16)
    ranks = draw_ranks(jax.random.fold_in(seeds[8], 71), 0)
    boards = draw_boards(jax.random.fold_in(seeds[8], 71), 0)
    river_live = draw_river_live(jax.random.fold_in(seeds[8], 71), 0)
    iso_weight = set_ends(jax.random.randint(seeds[5], (FLOPS,), 1, 25), jax.random.fold_in(seeds[5], 1), 1, 24).astype(jnp.int32)
    pot = jnp.clip(jnp.exp(jax.random.uniform(seeds[6], (LINES,), jnp.float32, math.log(2.0), math.log(24.0))), 2.0, 24.0)
    line_act = set_ends(jax.random.randint(seeds[7], (LINES,), 0, ACTS), jax.random.fold_in(seeds[7], 1), 0, ACTS - 1).astype(jnp.int32)
    return dict(reach_pre=reach_pre, strategy=strategy, ranks=ranks, boards=boards, river_live=river_live, iso_weight=iso_weight, pot=pot, line_act=line_act)


def card_tables():
    first_card, second_card = np.triu_indices(52, 1)
    padding = HPAD - HANDS
    first_card = np.concatenate([first_card, np.full(padding, 52)]).astype(np.int32)
    second_card = np.concatenate([second_card, np.full(padding, 53)]).astype(np.int32)
    alive_mask = np.concatenate([np.ones(HANDS), np.zeros(padding)]).astype(np.float32)
    return jnp.asarray(first_card), jnp.asarray(second_card), jnp.asarray(alive_mask)


def unblocked(first_rows, second_rows, first_cols, second_cols):
    clear = (first_rows[:, None] != first_cols[None, :]) & (first_rows[:, None] != second_cols[None, :])
    clear = clear & (second_rows[:, None] != first_cols[None, :]) & (second_rows[:, None] != second_cols[None, :])
    return clear.astype(jnp.float32)


def live_hands(first_card, second_card, alive_mask, board_cards):
    clear = jnp.all((first_card[:, None] != board_cards[None, :]) & (second_card[:, None] != board_cards[None, :]), axis=1)
    return alive_mask * clear.astype(jnp.float32)


def showdown(rank_rows, rank_cols, live_rows, live_cols, blocking):
    signed = jnp.sign(rank_rows[:, None] - rank_cols[None, :]).astype(jnp.float32)
    return (signed * blocking.astype(jnp.float32) * live_rows[:, None] * live_cols[None, :]).astype(jnp.bfloat16)


def reference(reach_pre, strategy, ranks, boards, river_live, iso_weight, pot, line_act):
    first_card, second_card, alive_mask = card_tables()
    total_reach = jnp.sum(reach_pre * alive_mask)
    blocking = unblocked(first_card, second_card, first_card, second_card).astype(jnp.bfloat16)
    onehot = (line_act[:, None] == jnp.arange(ACTS, dtype=jnp.int32)[None, :]).astype(jnp.float32)

    def per_flop(running, items):
        strat_flop, ranks_flop, boards_flop, count_flop, iso_flop = items
        line_reach = (reach_pre[None, :] * strat_flop.astype(jnp.float32) / total_reach).astype(jnp.bfloat16)

        def one_runout(runout, acc):
            live_now = live_hands(first_card, second_card, alive_mask, boards_flop[runout])
            matrix = showdown(ranks_flop[runout], ranks_flop[runout], live_now, live_now, blocking)
            values = jnp.dot(matrix, line_reach.T, preferred_element_type=jnp.float32)
            return acc + values * (runout < count_flop).astype(jnp.float32)

        acc = lax.fori_loop(0, RIV, one_runout, jnp.zeros((HPAD, LINES), jnp.float32))
        line_values = acc * pot[None, :] / count_flop.astype(jnp.float32)
        group_values = jnp.dot(line_values, onehot, precision=lax.Precision.HIGHEST, preferred_element_type=jnp.float32)
        best = jnp.max(group_values, axis=1)
        return running + iso_flop.astype(jnp.float32) * best, None

    summed, unused = lax.scan(per_flop, jnp.zeros((HPAD,), jnp.float32), (strategy, ranks, boards, river_live, iso_weight))
    return summed / jnp.sum(iso_weight.astype(jnp.float32))
```

```python
import functools

import jax
import jax.numpy as jnp
import numpy as np
from jax import lax
from jax.experimental import pallas as pl
from jax.experimental.pallas import tpu as pltpu
from jax.sharding import PartitionSpec as P

HANDS = 1326
HPAD = 1408
ACTS = 3
CARDS = 128
DEAD_CARD = 52
GROUP = 4
SPLITS = 3

VMEM = pl.BlockSpec(memory_space=pltpu.VMEM)
SMEM = pl.BlockSpec(memory_space=pltpu.SMEM)
NT = (((1,), (1,)), ((), ()))


def card_incidence():
    first_card, second_card = np.triu_indices(52, 1)
    padding = HPAD - HANDS
    first_card = np.concatenate([first_card, np.full(padding, 52)])
    second_card = np.concatenate([second_card, np.full(padding, 53)])
    table = np.zeros((HPAD, CARDS), np.float32)
    table[np.arange(HPAD), first_card] = 1
    table[np.arange(HPAD), second_card] = 1
    return jnp.asarray(table, jnp.bfloat16)


def params(cost=None, megabytes=48):
    return dict(
        compiler_params=pltpu.CompilerParams(vmem_limit_bytes=megabytes << 20),
        cost_estimate=cost,
    )


def showdown_kernel(
    hand_ref, count_ref, ranks_ref, boards_ref, cards_ref, sums_ref,
    rank_rows, live_rows, columns, spread, clear,
):
    flops, runouts = sums_ref.shape[0], rank_rows.shape[0] // sums_ref.shape[0]
    total = flops * runouts
    rows = sums_ref.shape[1]
    start = pl.multiple_of(hand_ref[0] * rows, 32)
    cards = cards_ref[...]
    own_cards = cards_ref[pl.ds(start, rows), :]

    card_ids = lax.broadcasted_iota(jnp.int32, (total, CARDS), 1)
    on_board = card_ids == DEAD_CARD
    boards = boards_ref[...]
    for place in range(boards.shape[1]):
        on_board = on_board | (card_ids == boards[:, place : place + 1])
    on_board = jnp.where(on_board, 1.0, 0.0).astype(jnp.bfloat16)

    ranks = ranks_ref[...].astype(jnp.float32)
    rank_rows[...] = ranks
    hits = lax.dot_general(on_board, cards, NT, preferred_element_type=jnp.float32)
    live_rows[...] = jnp.maximum(1.0 - hits, 0.0)

    columns[:, :total] = jnp.transpose(ranks, (1, 0))
    columns[:, total:] = jnp.transpose(live_rows[...], (1, 0))
    own_columns = columns[pl.ds(start, rows), :].astype(jnp.bfloat16)

    shared = lax.dot_general(own_cards, cards, NT, preferred_element_type=jnp.float32)
    clear[...] = jnp.maximum(1.0 - shared, 0.0).astype(jnp.bfloat16)

    pick_row = lax.broadcasted_iota(jnp.int32, (2 * total, 256), 0)
    pick_lane = lax.broadcasted_iota(jnp.int32, (2 * total, 256), 1)
    block = 16

    def add_runout(flop, runout, first):
        at = flop * runouts + runout
        pick = pick_row == jnp.where(pick_lane < 128, at, total + at)
        spread[...] = jnp.dot(
            own_columns,
            jnp.where(pick, 1.0, 0.0).astype(jnp.bfloat16),
            preferred_element_type=jnp.float32,
        ).astype(jnp.bfloat16)
        slots = rank_rows.shape[1]
        rank_j = jnp.broadcast_to(rank_rows[pl.ds(at, 1), :], (block, slots)).astype(jnp.bfloat16)
        live_j = jnp.broadcast_to(live_rows[pl.ds(at, 1), :], (block, slots)).astype(jnp.bfloat16)
        for part in range(rows // block):
            span = pl.ds(part * block, block)
            rank_i = spread[span, 0:128]
            live_i = spread[span, 128:256]
            for lane in range(0, slots, 128):
                lanes = pl.ds(lane, 128)
                sign = (rank_i - rank_j[:, lane : lane + 128]) * live_j[:, lane : lane + 128]
                sign = jnp.minimum(jnp.maximum(sign, -live_i), live_i)
                sign = sign * clear[span, lanes]
                if first:
                    sums_ref[flop, span, lanes] = sign
                else:
                    sums_ref[flop, span, lanes] += sign

    def one_flop(flop, carry):
        add_runout(flop, 0, True)

        def more(runout, carry):
            add_runout(flop, runout, False)
            return carry

        return lax.fori_loop(1, count_ref[flop], more, carry)

    lax.fori_loop(0, flops, one_flop, 0)


def showdown_sums(hand, counts, ranks, boards, cards, rows):
    flops, runouts, slots = ranks.shape
    total = flops * runouts
    return pl.pallas_call(
        showdown_kernel,
        out_shape=jax.ShapeDtypeStruct((flops, rows, slots), jnp.bfloat16),
        in_specs=[SMEM, SMEM, VMEM, VMEM, VMEM],
        out_specs=VMEM,
        scratch_shapes=[
            pltpu.VMEM((total, slots), jnp.float32),
            pltpu.VMEM((total, slots), jnp.float32),
            pltpu.VMEM((slots, 2 * total), jnp.float32),
            pltpu.VMEM((rows, 256), jnp.bfloat16),
            pltpu.VMEM((rows, slots), jnp.bfloat16),
        ],
        name="showdown_sums",
        **params(pl.CostEstimate(flops=4 * 10**9, bytes_accessed=10**7, transcendentals=0)),
    )(hand, counts, ranks.reshape(total, slots), boards.reshape(total, -1), cards)


def split_bf16(values):
    parts = []
    for _ in range(SPLITS):
        part = values.astype(jnp.bfloat16).astype(jnp.float32)
        parts.append(part)
        values = values - part
    return parts


def action_kernel(hand_ref, reach_ref, strategy_ref, pot_ref, act_ref, out_ref):
    flops, lines, rows = strategy_ref.shape
    senders, per = reach_ref.shape
    own = rows // per
    reach = reach_ref[...]
    slot = lax.broadcasted_iota(jnp.int32, (senders, per), 0) * per + lax.broadcasted_iota(
        jnp.int32, (senders, per), 1
    )
    alive = jnp.where(slot < HANDS, reach, 0.0)
    total = jnp.sum(jnp.sum(alive, axis=1, keepdims=True), axis=0, keepdims=True)

    mine = reach_ref[pl.ds(pl.multiple_of(hand_ref[0] * own, 8), own), :]
    lane = lax.broadcasted_iota(jnp.int32, (per, rows), 1)
    within = lax.broadcasted_iota(jnp.int32, (per, rows), 0)
    repeat = jnp.where(lax.rem(lane, per) == within, 1.0, 0.0)
    wide = jnp.dot(
        mine, repeat, precision=lax.Precision.HIGHEST, preferred_element_type=jnp.float32
    )
    row_lane = lax.broadcasted_iota(jnp.int32, (own, rows), 1)
    row_id = lax.broadcasted_iota(jnp.int32, (own, rows), 0)
    in_place = (row_lane >= row_id * per) & (row_lane < (row_id + 1) * per)
    own_reach = jnp.sum(jnp.where(in_place, wide, 0.0), axis=0, keepdims=True)
    scale = own_reach / total

    act = act_ref[...]
    row = lax.broadcasted_iota(jnp.int32, (8, lines), 0)
    weights = jnp.where(row == act, jnp.broadcast_to(pot_ref[...], (8, lines)), 0.0)
    weights = jnp.concatenate(split_bf16(weights), axis=0).astype(jnp.bfloat16)
    for flop in range(flops):
        line_reach = (strategy_ref[flop].astype(jnp.float32) * scale).astype(jnp.bfloat16)
        parts = jnp.dot(weights, line_reach, preferred_element_type=jnp.float32)
        sums = parts[0:8] + parts[8:16] + parts[16:24]
        out_ref[flop * GROUP : (flop + 1) * GROUP, :] = sums[0:GROUP]


def action_sums(hand, reach, strategy, pot, line_act):
    flops, lines, rows = strategy.shape
    return pl.pallas_call(
        action_kernel,
        out_shape=jax.ShapeDtypeStruct((flops * GROUP, rows), jnp.float32),
        in_specs=[SMEM, VMEM, VMEM, VMEM, VMEM],
        out_specs=VMEM,
        name="action_sums",
        **params(pl.CostEstimate(flops=10**8, bytes_accessed=10**6, transcendentals=0), 16),
    )(hand, reach, strategy, pot.reshape(1, lines), line_act.reshape(1, lines))


def response_kernel(hand_ref, count_ref, weight_ref, sums_ref, *refs):
    shards, (out_ref,) = refs[:-1], refs[-1:]
    flops, rows, slots = sums_ref.shape
    gathered = jnp.zeros((flops * GROUP, slots), jnp.float32)
    for step, shard in enumerate(shards):
        at = jnp.bitwise_xor(hand_ref[0], step) * rows
        piece = shard[...]
        empty = jnp.zeros((flops * GROUP, slots - rows), jnp.float32)
        gathered = gathered + pltpu.roll(jnp.concatenate([piece, empty], axis=1), at, 1)
    splits = split_bf16(gathered)
    values = jnp.zeros((1, rows), jnp.float32)
    weight_sum = 0
    for pair in range(flops * GROUP // 8):
        left = jnp.concatenate([part[pair * 8 : pair * 8 + 8] for part in splits], axis=0)
        left = left.astype(jnp.bfloat16)
        for flop in range(pair * 8 // GROUP, (pair + 1) * 8 // GROUP):
            parts = lax.dot_general(
                left, sums_ref[flop], NT, preferred_element_type=jnp.float32
            )
            group = parts[0:8] + parts[8:16] + parts[16:24]
            at = flop * GROUP - pair * 8
            best = jnp.max(group[at : at + ACTS], axis=0, keepdims=True)
            weight = weight_ref[flop]
            values = values + best * weight.astype(jnp.float32) / jnp.full(
                (1, rows), count_ref[flop].astype(jnp.float32)
            )
            weight_sum = weight_sum + weight
    tail = jnp.full((1, out_ref.shape[1] - rows), weight_sum.astype(jnp.float32))
    out_ref[...] = jnp.broadcast_to(jnp.concatenate([values, tail], axis=1), out_ref.shape)


def best_response(hand, counts, weights, sums, shards, copies):
    flops, rows, slots = sums.shape
    width = -(-(rows + 1) // 128) * 128
    return pl.pallas_call(
        response_kernel,
        out_shape=jax.ShapeDtypeStruct((copies, width), jnp.float32),
        in_specs=[SMEM, SMEM, SMEM] + [VMEM] * (1 + len(shards)),
        out_specs=VMEM,
        name="best_response",
        **params(pl.CostEstimate(flops=10**9, bytes_accessed=10**7, transcendentals=0)),
    )(hand, counts, weights, sums, *shards)


def body(boards_n, hands_n, reach_pre, strategy, ranks, boards, river_live, iso_weight, pot, line_act):
    everyone = ("board", "hand")
    flops, lines, rows = strategy.shape
    hand = lax.axis_index("hand").astype(jnp.int32).reshape(1)
    devices = boards_n * hands_n

    copies = jnp.broadcast_to(reach_pre[None, :], (devices, reach_pre.shape[0]))
    reach = lax.all_to_all(copies, everyone, 0, 0, tiled=True)
    sums = showdown_sums(hand, river_live, ranks, boards, card_incidence(), rows)

    grouped = action_sums(hand, reach, strategy, pot, line_act)
    shards = [grouped]
    for step in range(1, hands_n):
        swap = [(source, source ^ step) for source in range(hands_n)]
        shards.append(lax.ppermute(grouped, "hand", swap))

    partial = best_response(hand, river_live, iso_weight, sums, shards, boards_n)
    parts = lax.all_to_all(partial, "board", 0, 0, tiled=True)
    whole = jnp.sum(parts, axis=0)
    return whole[:rows] / whole[rows]


def solution(mesh):
    in_specs = (
        P(("board", "hand")),
        P("board", None, "hand"),
        P("board", None, None),
        P("board", None, None),
        P("board"),
        P("board"),
        P(),
        P(),
    )
    run = functools.partial(body, mesh.shape["board"], mesh.shape["hand"])
    return jax.shard_map(run, mesh=mesh, in_specs=in_specs, out_specs=P("hand"), check_vma=False)
```

```python
import functools

import jax
import jax.numpy as jnp
import numpy as np
from jax import lax
from jax.experimental import pallas as pl
from jax.experimental.pallas import tpu as pltpu
from jax.sharding import PartitionSpec as P

HANDS = 1326
HPAD = 1408
ACTS = 3
CARDS = 128
DEAD_CARD = 52
GROUP = 4
SPLITS = 3
RANKS = 128
USED_RANKS = 96
NO_RANK = 127.0

VMEM = pl.BlockSpec(memory_space=pltpu.VMEM)
SMEM = pl.BlockSpec(memory_space=pltpu.SMEM)
NT = (((1,), (1,)), ((), ()))
TN = (((0,), (0,)), ((), ()))
EXACT = jnp.float8_e4m3fn


def card_incidence():
    first_card, second_card = np.triu_indices(52, 1)
    padding = HPAD - HANDS
    first_card = np.concatenate([first_card, np.full(padding, 52)])
    second_card = np.concatenate([second_card, np.full(padding, 53)])
    table = np.zeros((HPAD, CARDS), np.float32)
    table[np.arange(HPAD), first_card] = 1
    table[np.arange(HPAD), second_card] = 1
    return jnp.asarray(table, jnp.bfloat16)


def params(cost=None, megabytes=48):
    return dict(
        compiler_params=pltpu.CompilerParams(vmem_limit_bytes=megabytes << 20),
        cost_estimate=cost,
    )


def showdown_kernel(
    hand_ref, count_ref, ranks_ref, boards_ref, cards_ref, sums_ref,
    rank_rows, own_rows, live_rows, clear, holds, signs,
):
    flops, slots, rows = sums_ref.shape
    total = rank_rows.shape[0]
    runouts = total // flops
    start = pl.multiple_of(hand_ref[0] * rows, 32)
    cards = cards_ref[...]
    own_cards = cards_ref[pl.ds(start, rows), :]

    card_ids = lax.broadcasted_iota(jnp.int32, (total, CARDS), 1)
    on_board = card_ids == DEAD_CARD
    boards = boards_ref[...]
    for place in range(boards.shape[1]):
        on_board = on_board | (card_ids == boards[:, place : place + 1])
    on_board = jnp.where(on_board, 1.0, 0.0).astype(jnp.bfloat16)

    hits = lax.dot_general(on_board, cards, NT, preferred_element_type=jnp.float32)
    ranks = jnp.where(hits > 0.0, NO_RANK, ranks_ref[...].astype(jnp.float32))
    rank_rows[...] = ranks
    own_ranks = pltpu.roll(ranks, lax.rem(slots - start, slots), 1)[:, :rows]
    own_rows[...] = own_ranks
    live_rows[...] = jnp.where(own_ranks < NO_RANK, 1.0, 0.0)

    shared = lax.dot_general(cards, own_cards, NT, preferred_element_type=jnp.float32)
    clear[...] = jnp.maximum(1.0 - shared, 0.0).astype(jnp.bfloat16)
    holds[...] = jnp.zeros_like(holds)
    signs[...] = jnp.zeros_like(signs)

    def level(width):
        return lax.broadcasted_iota(jnp.int32, (USED_RANKS, width), 0).astype(jnp.float32)

    def add_runout(at, low):
        span = pl.ds(pl.multiple_of(low, RANKS), USED_RANKS)
        rank = rank_rows[pl.ds(at, 1), :]
        holds[span, :] = jnp.where(rank == level(slots), 1.0, 0.0).astype(EXACT)
        sign = jnp.minimum(jnp.maximum(own_rows[pl.ds(at, 1), :] - level(rows), -1.0), 1.0)
        signs[span, :] = (sign * live_rows[pl.ds(at, 1), :]).astype(EXACT)

    def multiply(flop, depth):
        right = signs[:depth, :]
        for lane in range(0, slots, 256):
            part = slice(lane, min(lane + 256, slots))
            sign = lax.dot_general(holds[:depth, part], right, TN, preferred_element_type=jnp.float32)
            sums_ref[flop, part, :] = sign.astype(jnp.bfloat16) * clear[part, :]

    def one_flop(flop, carry):
        count = count_ref[flop]

        def one_runout(runout, carry):
            add_runout(flop * runouts + runout, runout * RANKS)
            return carry

        lax.fori_loop(0, count, one_runout, 0)
        even = lax.rem(count, 2) == 0

        @pl.when(jnp.logical_not(even) & (count > 1))
        def _():
            empty = jnp.zeros((RANKS, rows), EXACT)
            signs[pl.ds(pl.multiple_of(count * RANKS, RANKS), RANKS), :] = empty

        @pl.when(count == 1)
        def _():
            multiply(flop, RANKS)

        for step in range(2, runouts + 1, 2):

            @pl.when((count == step) | ((count == step - 1) & (count > 1)))
            def _():
                multiply(flop, step * RANKS)

        return carry

    lax.fori_loop(0, flops, one_flop, 0)


def showdown_sums(hand, counts, ranks, boards, cards, rows):
    flops, runouts, slots = ranks.shape
    total = flops * runouts
    return pl.pallas_call(
        showdown_kernel,
        out_shape=jax.ShapeDtypeStruct((flops, slots, rows), jnp.bfloat16),
        in_specs=[SMEM, SMEM, VMEM, VMEM, VMEM],
        out_specs=VMEM,
        scratch_shapes=[
            pltpu.VMEM((total, slots), jnp.float32),
            pltpu.VMEM((total, rows), jnp.float32),
            pltpu.VMEM((total, rows), jnp.float32),
            pltpu.VMEM((slots, rows), jnp.bfloat16),
            pltpu.VMEM((runouts * RANKS, slots), EXACT),
            pltpu.VMEM((runouts * RANKS, rows), EXACT),
        ],
        name="showdown_sums",
        **params(pl.CostEstimate(flops=4 * 10**9, bytes_accessed=10**7, transcendentals=0), 18),
    )(hand, counts, ranks.reshape(total, slots), boards.reshape(total, -1), cards)


def split_bf16(values):
    parts = []
    for _ in range(SPLITS):
        part = values.astype(jnp.bfloat16).astype(jnp.float32)
        parts.append(part)
        values = values - part
    return parts


def action_kernel(hand_ref, reach_ref, strategy_ref, pot_ref, act_ref, out_ref):
    flops, lines, rows = strategy_ref.shape
    senders, per = reach_ref.shape
    own = rows // per
    reach = reach_ref[...]
    slot = lax.broadcasted_iota(jnp.int32, (senders, per), 0) * per + lax.broadcasted_iota(
        jnp.int32, (senders, per), 1
    )
    alive = jnp.where(slot < HANDS, reach, 0.0)
    total = jnp.sum(jnp.sum(alive, axis=1, keepdims=True), axis=0, keepdims=True)

    mine = reach_ref[pl.ds(pl.multiple_of(hand_ref[0] * own, 8), own), :]
    lane = lax.broadcasted_iota(jnp.int32, (per, rows), 1)
    within = lax.broadcasted_iota(jnp.int32, (per, rows), 0)
    repeat = jnp.where(lax.rem(lane, per) == within, 1.0, 0.0)
    wide = jnp.dot(
        mine, repeat, precision=lax.Precision.HIGHEST, preferred_element_type=jnp.float32
    )
    row_lane = lax.broadcasted_iota(jnp.int32, (own, rows), 1)
    row_id = lax.broadcasted_iota(jnp.int32, (own, rows), 0)
    in_place = (row_lane >= row_id * per) & (row_lane < (row_id + 1) * per)
    own_reach = jnp.sum(jnp.where(in_place, wide, 0.0), axis=0, keepdims=True)
    scale = own_reach / total

    act = act_ref[...]
    row = lax.broadcasted_iota(jnp.int32, (8, lines), 0)
    weights = jnp.where(row == act, jnp.broadcast_to(pot_ref[...], (8, lines)), 0.0)
    weights = jnp.concatenate(split_bf16(weights), axis=0).astype(jnp.bfloat16)
    for flop in range(flops):
        line_reach = (strategy_ref[flop].astype(jnp.float32) * scale).astype(jnp.bfloat16)
        parts = jnp.dot(weights, line_reach, preferred_element_type=jnp.float32)
        sums = parts[0:8] + parts[8:16] + parts[16:24]
        out_ref[flop * GROUP : (flop + 1) * GROUP, :] = sums[0:GROUP]


def action_sums(hand, reach, strategy, pot, line_act):
    flops, lines, rows = strategy.shape
    return pl.pallas_call(
        action_kernel,
        out_shape=jax.ShapeDtypeStruct((flops * GROUP, rows), jnp.float32),
        in_specs=[SMEM, VMEM, VMEM, VMEM, VMEM],
        out_specs=VMEM,
        name="action_sums",
        **params(pl.CostEstimate(flops=10**8, bytes_accessed=10**6, transcendentals=0), 16),
    )(hand, reach, strategy, pot.reshape(1, lines), line_act.reshape(1, lines))


def response_kernel(hand_ref, count_ref, weight_ref, sums_ref, *refs):
    shards, (out_ref,) = refs[:-1], refs[-1:]
    flops, slots, rows = sums_ref.shape
    gathered = jnp.zeros((flops * GROUP, slots), jnp.float32)
    for step, shard in enumerate(shards):
        at = jnp.bitwise_xor(hand_ref[0], step) * rows
        piece = shard[...]
        empty = jnp.zeros((flops * GROUP, slots - rows), jnp.float32)
        gathered = gathered + pltpu.roll(jnp.concatenate([piece, empty], axis=1), at, 1)
    splits = split_bf16(gathered)
    values = jnp.zeros((1, rows), jnp.float32)
    weight_sum = 0
    for pair in range(flops * GROUP // 8):
        left = jnp.concatenate([part[pair * 8 : pair * 8 + 8] for part in splits], axis=0)
        left = left.astype(jnp.bfloat16)
        for flop in range(pair * 8 // GROUP, (pair + 1) * 8 // GROUP):
            parts = jnp.dot(left, sums_ref[flop], preferred_element_type=jnp.float32)
            group = parts[0:8] + parts[8:16] + parts[16:24]
            at = flop * GROUP - pair * 8
            best = jnp.max(group[at : at + ACTS], axis=0, keepdims=True)
            weight = weight_ref[flop]
            values = values + best * weight.astype(jnp.float32) / jnp.full(
                (1, rows), count_ref[flop].astype(jnp.float32)
            )
            weight_sum = weight_sum + weight
    tail = jnp.full((1, out_ref.shape[1] - rows), weight_sum.astype(jnp.float32))
    out_ref[...] = jnp.broadcast_to(jnp.concatenate([values, tail], axis=1), out_ref.shape)


def best_response(hand, counts, weights, sums, shards, copies):
    flops, slots, rows = sums.shape
    width = -(-(rows + 1) // 128) * 128
    return pl.pallas_call(
        response_kernel,
        out_shape=jax.ShapeDtypeStruct((copies, width), jnp.float32),
        in_specs=[SMEM, SMEM, SMEM] + [VMEM] * (1 + len(shards)),
        out_specs=VMEM,
        name="best_response",
        **params(pl.CostEstimate(flops=10**9, bytes_accessed=10**7, transcendentals=0), 12),
    )(hand, counts, weights, sums, *shards)


def body(boards_n, hands_n, reach_pre, strategy, ranks, boards, river_live, iso_weight, pot, line_act):
    everyone = ("board", "hand")
    flops, lines, rows = strategy.shape
    hand = lax.axis_index("hand").astype(jnp.int32).reshape(1)
    devices = boards_n * hands_n

    copies = jnp.broadcast_to(reach_pre[None, :], (devices, reach_pre.shape[0]))
    reach = lax.all_to_all(copies, everyone, 0, 0, tiled=True)
    sums = showdown_sums(hand, river_live, ranks, boards, card_incidence(), rows)

    grouped = action_sums(hand, reach, strategy, pot, line_act)
    shards = [grouped]
    for step in range(1, hands_n):
        swap = [(source, source ^ step) for source in range(hands_n)]
        shards.append(lax.ppermute(grouped, "hand", swap))

    partial = best_response(hand, river_live, iso_weight, sums, shards, boards_n)
    parts = lax.all_to_all(partial, "board", 0, 0, tiled=True)
    whole = jnp.sum(parts, axis=0)
    return whole[:rows] / whole[rows]


def solution(mesh):
    in_specs = (
        P(("board", "hand")),
        P("board", None, "hand"),
        P("board", None, None),
        P("board", None, None),
        P("board"),
        P("board"),
        P(),
        P(),
    )
    run = functools.partial(body, mesh.shape["board"], mesh.shape["hand"])
    return jax.shard_map(run, mesh=mesh, in_specs=in_specs, out_specs=P("hand"), check_vma=False)
```

```python
import functools

import jax
import jax.numpy as jnp
import numpy as np
from jax import lax
from jax.experimental import pallas as pl
from jax.experimental.pallas import tpu as pltpu
from jax.sharding import PartitionSpec as P

HANDS = 1326
HPAD = 1408
ACTS = 3
CARDS = 64
DEAD_CARD = 52
GROUP = 4
SPLITS = 3
PART = 4
FAR = 40
FAR_FLOPS = 24
RANKS = 128
USED_RANKS = 96
NO_RANK = 127.0

VMEM = pl.BlockSpec(memory_space=pltpu.VMEM)
SMEM = pl.BlockSpec(memory_space=pltpu.SMEM)
ANY = pl.BlockSpec(memory_space=pltpu.HBM)
NT = (((1,), (1,)), ((), ()))
TN = (((0,), (0,)), ((), ()))
EXACT = jnp.float8_e4m3fn


def hand_cards():
    first_card, second_card = np.triu_indices(52, 1)
    padding = HPAD - HANDS
    first_card = np.concatenate([first_card, np.full(padding, 52)])
    second_card = np.concatenate([second_card, np.full(padding, 53)])
    return jnp.asarray(np.stack([first_card, second_card]), jnp.int32)


def params(megabytes, flops=0, moved=10**6):
    return dict(
        compiler_params=pltpu.CompilerParams(vmem_limit_bytes=megabytes << 20),
        cost_estimate=pl.CostEstimate(flops=flops, bytes_accessed=moved, transcendentals=0),
    )


def copies_kernel(reach_ref, send_ref):
    send_ref[...] = jnp.broadcast_to(reach_ref[...], send_ref.shape)


def reach_copies(devices, reach):
    per = reach.shape[0]
    return pl.pallas_call(
        copies_kernel,
        out_shape=jax.ShapeDtypeStruct((devices, per), jnp.float32),
        in_specs=[VMEM],
        out_specs=VMEM,
        name="reach_copies",
        **params(1, 10**10, 10**8),
    )(reach.reshape(1, per))


def level(width):
    return lax.broadcasted_iota(jnp.int32, (USED_RANKS, width), 0).astype(jnp.float32)


def add_flops(first, last, count_ref, rank_rows, own_rows, live_rows, clear, holds, signs, sums_ref, sent):
    slots, rows = clear.shape
    runouts = holds.shape[0] // RANKS
    for low in range(0, runouts * RANKS, RANKS):
        holds[low + USED_RANKS : low + RANKS, :] = jnp.zeros((RANKS - USED_RANKS, slots), EXACT)
        signs[low + USED_RANKS : low + RANKS, :] = jnp.zeros((RANKS - USED_RANKS, rows), EXACT)

    def add_runout(at, low):
        span = pl.ds(pl.multiple_of(low, RANKS), USED_RANKS)
        rank = rank_rows[pl.ds(at, 1), :]
        holds[span, :] = jnp.where(rank == level(slots), 1.0, 0.0).astype(EXACT)
        sign = jnp.minimum(jnp.maximum(own_rows[pl.ds(at, 1), :] - level(rows), -1.0), 1.0)
        signs[span, :] = (sign * live_rows[pl.ds(at, 1), :]).astype(EXACT)

    def multiply(flop, depth):
        right = signs[:depth, :]
        for lane in range(0, slots, 256):
            part = slice(lane, min(lane + 256, slots))
            sign = lax.dot_general(holds[:depth, part], right, TN, preferred_element_type=jnp.float32)
            sums_ref[flop, part, :] = sign.astype(jnp.bfloat16) * clear[part, :]

    def one_flop(flop, carry):
        count = count_ref[flop]

        def one_runout(runout, carry):
            add_runout(flop * runouts + runout, runout * RANKS)
            return carry

        lax.fori_loop(0, count, one_runout, 0)

        @pl.when((lax.rem(count, 2) == 1) & (count > 1))
        def _():
            span = pl.ds(pl.multiple_of(count * RANKS, RANKS), RANKS)
            holds[span, :] = jnp.zeros((RANKS, slots), EXACT)
            signs[span, :] = jnp.zeros((RANKS, rows), EXACT)

        @pl.when(count == 1)
        def _():
            multiply(flop, RANKS)

        for step in range(2, runouts + 1, 2):

            @pl.when((count == step) | ((count == step - 1) & (count > 1)))
            def _():
                multiply(flop, step * RANKS)

        sent(flop)
        return carry

    lax.fori_loop(first, last, one_flop, 0)


def first_kernel(
    count_ref, ranks_ref, boards_ref, cards_ref, pot_ref, act_ref,
    far_ref, rank_rows, own_rows, live_rows, clear, weights_ref, holds, signs, sums, sem,
):
    slots, rows = clear.shape
    total = ranks_ref.shape[0]
    places, flops, runouts = boards_ref.shape
    start = lax.axis_index("hand") * rows
    turn = lax.rem(slots - start, slots)

    cards = cards_ref[...]
    own_cards = pltpu.roll(cards, turn, 1)[:, :rows]
    card = lax.broadcasted_iota(jnp.int32, (CARDS, slots), 0)
    holders = jnp.where((card == cards[0:1]) | (card == cards[1:2]), 1.0, 0.0).astype(EXACT)
    card = lax.broadcasted_iota(jnp.int32, (CARDS, rows), 0)
    own_holders = (card == own_cards[0:1]) | (card == own_cards[1:2])
    own_holders = jnp.where(own_holders, 1.0, 0.0).astype(EXACT)

    boards = jnp.concatenate([boards_ref[place] for place in range(places)], axis=1)
    row = lax.broadcasted_iota(jnp.int32, (total, flops), 0)
    of_flop = row // runouts == lax.broadcasted_iota(jnp.int32, (total, flops), 1)
    spread = jnp.dot(
        jnp.where(of_flop, 1.0, 0.0).astype(jnp.bfloat16),
        boards.astype(jnp.float32).astype(jnp.bfloat16),
        preferred_element_type=jnp.float32,
    )
    row = lax.broadcasted_iota(jnp.int32, spread.shape, 0)
    lane = lax.broadcasted_iota(jnp.int32, spread.shape, 1)
    mine = lax.rem(row, runouts) == lax.rem(lane, runouts)
    card = lax.broadcasted_iota(jnp.int32, (total, CARDS), 1)
    on_board = card == DEAD_CARD
    for place in range(places):
        here = mine & (lane // runouts == place)
        found = jnp.sum(jnp.where(here, spread, 0.0), axis=1, keepdims=True)
        on_board = on_board | (card.astype(jnp.float32) == found)
    on_board = jnp.where(on_board, 1.0, 0.0).astype(EXACT)

    hits = jnp.dot(on_board, holders, preferred_element_type=jnp.float32)
    ranks = jnp.where(hits > 0.0, NO_RANK, ranks_ref[...].astype(jnp.float32))
    rank_rows[...] = ranks
    own_ranks = pltpu.roll(ranks, turn, 1)[:, :rows]
    own_rows[...] = own_ranks
    live_rows[...] = jnp.where(own_ranks < NO_RANK, 1.0, 0.0)

    shared = lax.dot_general(holders, own_holders, TN, preferred_element_type=jnp.float32)
    clear[...] = jnp.maximum(1.0 - shared, 0.0).astype(jnp.bfloat16)

    act = act_ref[...]
    row = lax.broadcasted_iota(jnp.int32, (8, act.shape[1]), 0)
    weights = jnp.where(row == act, jnp.broadcast_to(pot_ref[...], row.shape), 0.0)
    weights_ref[...] = jnp.concatenate(split_bf16(weights), axis=0).astype(jnp.bfloat16)

    def copy(flop):
        return pltpu.make_async_copy(sums.at[flop], far_ref.at[flop], sem.at[flop])

    part = sums.shape[0]
    tables = (count_ref, rank_rows, own_rows, live_rows, clear, holds, signs)
    add_flops(0, part, *tables, sums, lambda flop: copy(flop).start())
    for flop in range(part):
        copy(flop).wait()


def showdown_scratch(runouts, slots, rows):
    return [
        pltpu.VMEM((runouts * RANKS, slots), EXACT),
        pltpu.VMEM((runouts * RANKS, rows), EXACT),
    ]


def first_flops(part, counts, ranks, boards, cards, pot, line_act, rows):
    total, slots = ranks.shape
    flops, lines = counts.shape[0], pot.shape[1]
    return pl.pallas_call(
        first_kernel,
        out_shape=[
            jax.ShapeDtypeStruct((FAR_FLOPS, slots, rows), jnp.bfloat16),
            jax.ShapeDtypeStruct((total, slots), jnp.float32),
            jax.ShapeDtypeStruct((total, rows), jnp.float32),
            jax.ShapeDtypeStruct((total, rows), jnp.float32),
            jax.ShapeDtypeStruct((slots, rows), jnp.bfloat16),
            jax.ShapeDtypeStruct((8 * SPLITS, lines), jnp.bfloat16),
        ],
        in_specs=[SMEM] + [VMEM] * 5,
        out_specs=[ANY] + [VMEM] * 5,
        scratch_shapes=showdown_scratch(total // flops, slots, rows)
        + [pltpu.VMEM((part, slots, rows), jnp.bfloat16), pltpu.SemaphoreType.DMA((part,))],
        name="first_flops",
        **params(FAR, 2 * 10**9, 10**7),
    )(counts, ranks, boards, cards, pot, line_act)


def other_kernel(
    part, count_ref, rank_rows, own_rows, live_rows, clear, grouped_ref, far_ref, sums_ref,
    holds, signs, sem,
):
    copies = [
        pltpu.make_async_copy(far_ref.at[flop], sums_ref.at[flop], sem.at[flop])
        for flop in range(part)
    ]
    for copy in copies:
        copy.start()
    tables = (count_ref, rank_rows, own_rows, live_rows, clear, holds, signs)
    add_flops(part, sums_ref.shape[0], *tables, sums_ref, lambda flop: None)
    for copy in copies:
        copy.wait()


def other_flops(part, counts, rank_rows, own_rows, live_rows, clear, grouped, far):
    slots, rows = clear.shape
    flops = counts.shape[0]
    return pl.pallas_call(
        functools.partial(other_kernel, part),
        out_shape=jax.ShapeDtypeStruct((flops, slots, rows), jnp.bfloat16),
        in_specs=[SMEM, VMEM, VMEM, VMEM, VMEM, ANY, ANY],
        out_specs=VMEM,
        scratch_shapes=showdown_scratch(rank_rows.shape[0] // flops, slots, rows)
        + [pltpu.SemaphoreType.DMA((part,))],
        name="other_flops",
        **params(FAR, 2 * 10**9, 10**7),
    )(counts, rank_rows, own_rows, live_rows, clear, grouped, far)


def split_bf16(values):
    parts = []
    for _ in range(SPLITS):
        part = values.astype(jnp.bfloat16).astype(jnp.float32)
        parts.append(part)
        values = values - part
    return parts


def action_kernel(reach_ref, strategy_ref, weights_ref, out_ref):
    flops, rows, lines = strategy_ref.shape
    senders, per = reach_ref.shape
    own = rows // per
    reach = reach_ref[...]
    slot = lax.broadcasted_iota(jnp.int32, (senders, per), 0) * per + lax.broadcasted_iota(
        jnp.int32, (senders, per), 1
    )
    alive = jnp.where(slot < HANDS, reach, 0.0)
    total = jnp.sum(jnp.sum(alive, axis=1, keepdims=True), axis=0, keepdims=True)

    mine = reach_ref[pl.ds(pl.multiple_of(lax.axis_index("hand") * own, 8), own), :]
    row = lax.broadcasted_iota(jnp.int32, (rows, own), 0)
    low = lax.broadcasted_iota(jnp.int32, (rows, own), 1) * per
    sender = jnp.where((row >= low) & (row < low + per), 1.0, 0.0)
    wide = jnp.dot(
        sender, mine, precision=lax.Precision.HIGHEST, preferred_element_type=jnp.float32
    )
    row = lax.broadcasted_iota(jnp.int32, (rows, per), 0)
    lane = lax.broadcasted_iota(jnp.int32, (rows, per), 1)
    own_reach = jnp.sum(jnp.where(lax.rem(row, per) == lane, wide, 0.0), axis=1, keepdims=True)
    scale = jnp.broadcast_to(own_reach / total, (rows, lines))

    weights = weights_ref[...]
    for flop in range(flops):
        line_reach = (strategy_ref[flop].astype(jnp.float32) * scale).astype(jnp.bfloat16)
        parts = lax.dot_general(weights, line_reach, NT, preferred_element_type=jnp.float32)
        sums = parts[0:8] + parts[8:16] + parts[16:24]
        out_ref[flop * GROUP : (flop + 1) * GROUP, :] = sums[0:GROUP]


def action_sums(reach, strategy, weights):
    flops, rows, lines = strategy.shape
    return pl.pallas_call(
        action_kernel,
        out_shape=jax.ShapeDtypeStruct((flops * GROUP, rows), jnp.float32),
        in_specs=[VMEM] * 3,
        out_specs=VMEM,
        name="action_sums",
        **params(4, 10**8),
    )(reach, strategy, weights)


def response_kernel(count_ref, weight_ref, sums_ref, *refs):
    shards, out_ref = refs[:-1], refs[-1]
    flops, slots, rows = sums_ref.shape
    gathered = jnp.zeros((flops * GROUP, slots), jnp.float32)
    for step, shard in enumerate(shards):
        at = jnp.bitwise_xor(lax.axis_index("hand"), step) * rows
        empty = jnp.zeros((flops * GROUP, slots - rows), jnp.float32)
        gathered = gathered + pltpu.roll(jnp.concatenate([shard[...], empty], axis=1), at, 1)
    splits = split_bf16(gathered)
    values = jnp.zeros((1, rows), jnp.float32)
    weight_sum = 0
    for flop in range(flops):
        low = flop * GROUP // 8 * 8
        left = jnp.concatenate([part[low : low + 8] for part in splits], axis=0)
        parts = jnp.dot(
            left.astype(jnp.bfloat16), sums_ref[flop], preferred_element_type=jnp.float32
        )
        group = parts[0:8] + parts[8:16] + parts[16:24]
        at = flop * GROUP - low
        best = jnp.max(group[at : at + ACTS], axis=0, keepdims=True)
        weight = weight_ref[flop]
        count = jnp.full((1, rows), count_ref[flop].astype(jnp.float32))
        values = values + best * weight.astype(jnp.float32) / count
        weight_sum = weight_sum + weight
    tail = jnp.full((1, out_ref.shape[1] - rows), weight_sum.astype(jnp.float32))
    out_ref[...] = jnp.broadcast_to(jnp.concatenate([values, tail], axis=1), out_ref.shape)


def best_response(counts, weights, sums, shards, copies):
    rows = sums.shape[2]
    width = -(-(rows + 1) // 128) * 128
    return pl.pallas_call(
        response_kernel,
        out_shape=jax.ShapeDtypeStruct((copies, width), jnp.float32),
        in_specs=[SMEM, SMEM] + [VMEM] * (1 + len(shards)),
        out_specs=VMEM,
        name="best_response",
        **params(12, 10**9, 10**7),
    )(counts, weights, sums, *shards)


def finish_kernel(parts_ref, out_ref):
    rows = out_ref.shape[0]
    whole = jnp.sum(parts_ref[...], axis=0)
    weight = whole[rows : rows + 1]
    out_ref[...] = whole[:rows] / weight


def finish(parts, rows):
    return pl.pallas_call(
        finish_kernel,
        out_shape=jax.ShapeDtypeStruct((rows,), jnp.float32),
        in_specs=[VMEM],
        out_specs=VMEM,
        name="finish",
        **params(2),
    )(parts)


def body(boards_n, hands_n, reach_pre, strategy, ranks, boards, river_live, iso_weight, pot, line_act):
    lines, rows = strategy.shape[1:]
    flops, runouts, slots = ranks.shape
    part = PART

    send = reach_copies(boards_n * hands_n, reach_pre)
    reach = lax.all_to_all(send, ("board", "hand"), 0, 0, tiled=True)
    far, *near, weights = first_flops(
        part,
        river_live,
        ranks.reshape(flops * runouts, slots),
        jnp.transpose(boards, (2, 0, 1)),
        hand_cards(),
        pot.reshape(1, lines),
        line_act.reshape(1, lines),
        rows,
    )

    grouped = action_sums(reach, jnp.swapaxes(strategy, 1, 2), weights)
    shards = [grouped]
    for step in range(1, hands_n):
        swap = [(source, source ^ step) for source in range(hands_n)]
        shards.append(lax.ppermute(grouped, "hand", swap))
    sums = other_flops(part, river_live, *near, grouped, far)

    partial = best_response(river_live, iso_weight, sums, shards, boards_n)
    return finish(lax.all_to_all(partial, "board", 0, 0, tiled=True), rows)


def solution(mesh):
    in_specs = (
        P(("board", "hand")),
        P("board", None, "hand"),
        P("board", None, None),
        P("board", None, None),
        P("board"),
        P("board"),
        P(),
        P(),
    )
    run = functools.partial(body, mesh.shape["board"], mesh.shape["hand"])
    return jax.shard_map(run, mesh=mesh, in_specs=in_specs, out_specs=P("hand"), check_vma=False)
```

```python
import functools

import jax
import jax.numpy as jnp
import numpy as np
from jax import lax
from jax.experimental import pallas as pl
from jax.experimental.pallas import tpu as pltpu
from jax.sharding import PartitionSpec as P

HANDS = 1326
HPAD = 1408
ACTS = 3
CARDS = 64
DEAD_CARD = 52
GROUP = 4
SPLITS = 3
PART = 4
FAR = 40
FAR_FLOPS = 24
RANKS = 128
USED_RANKS = 96
NO_RANK = 127.0

VMEM = pl.BlockSpec(memory_space=pltpu.VMEM)
SMEM = pl.BlockSpec(memory_space=pltpu.SMEM)
ANY = pl.BlockSpec(memory_space=pltpu.HBM)
NT = (((1,), (1,)), ((), ()))
TN = (((0,), (0,)), ((), ()))
EXACT = jnp.float8_e4m3fn


def hand_cards():
    first_card, second_card = np.triu_indices(52, 1)
    padding = HPAD - HANDS
    first_card = np.concatenate([first_card, np.full(padding, 52)])
    second_card = np.concatenate([second_card, np.full(padding, 53)])
    return jnp.asarray(np.stack([first_card, second_card]), jnp.int32)


def params(megabytes, flops=0, moved=10**6):
    return dict(
        compiler_params=pltpu.CompilerParams(vmem_limit_bytes=megabytes << 20),
        cost_estimate=pl.CostEstimate(flops=flops, bytes_accessed=moved, transcendentals=0),
    )


def copies_kernel(reach_ref, send_ref):
    send_ref[...] = jnp.broadcast_to(reach_ref[...], send_ref.shape)


def reach_copies(devices, reach):
    per = reach.shape[0]
    return pl.pallas_call(
        copies_kernel,
        out_shape=jax.ShapeDtypeStruct((devices, per), jnp.float32),
        in_specs=[VMEM],
        out_specs=VMEM,
        name="reach_copies",
        **params(1, 10**10, 10**8),
    )(reach.reshape(1, per))


def level(width):
    return lax.broadcasted_iota(jnp.int32, (USED_RANKS, width), 0).astype(jnp.float32)


def add_flops(first, last, count_ref, rank_rows, own_rows, clear, holds, signs, sums_ref, sent):
    slots, rows = clear.shape
    runouts = holds.shape[0] // RANKS
    for low in range(0, runouts * RANKS, RANKS):
        holds[low + USED_RANKS : low + RANKS, :] = jnp.zeros((RANKS - USED_RANKS, slots), EXACT)
        signs[low + USED_RANKS : low + RANKS, :] = jnp.zeros((RANKS - USED_RANKS, rows), EXACT)

    def add_runout(at, low):
        span = pl.ds(pl.multiple_of(low, RANKS), USED_RANKS)
        rank = rank_rows[pl.ds(at, 1), :]
        holds[span, :] = jnp.where(rank == level(slots), 1.0, 0.0).astype(EXACT)
        rank = own_rows[pl.ds(at, 1), :]
        live = jnp.where(rank < NO_RANK, 1.0, 0.0)
        sign = jnp.minimum(jnp.maximum(rank - level(rows), -1.0), 1.0)
        signs[span, :] = (sign * live).astype(EXACT)

    def multiply(flop, depth):
        right = signs[:depth, :]
        for lane in range(0, slots, 256):
            part = slice(lane, min(lane + 256, slots))
            sign = lax.dot_general(holds[:depth, part], right, TN, preferred_element_type=jnp.float32)
            sums_ref[flop, part, :] = sign.astype(jnp.bfloat16) * clear[part, :]

    def one_flop(flop, carry):
        count = count_ref[flop]

        def one_runout(runout, carry):
            add_runout((flop - first) * runouts + runout, runout * RANKS)
            return carry

        lax.fori_loop(0, count, one_runout, 0)

        @pl.when((lax.rem(count, 2) == 1) & (count > 1))
        def _():
            span = pl.ds(pl.multiple_of(count * RANKS, RANKS), RANKS)
            holds[span, :] = jnp.zeros((RANKS, slots), EXACT)
            signs[span, :] = jnp.zeros((RANKS, rows), EXACT)

        @pl.when(count == 1)
        def _():
            multiply(flop, RANKS)

        for step in range(2, runouts + 1, 2):

            @pl.when((count == step) | ((count == step - 1) & (count > 1)))
            def _():
                multiply(flop, step * RANKS)

        sent(flop)
        return carry

    lax.fori_loop(first, last, one_flop, 0)


def first_kernel(
    count_ref, ranks_ref, boards_ref, cards_ref, pot_ref, act_ref,
    far_ref, near_ref, late_ranks, late_own, clear, weights_ref,
    holds, signs, rank_rows, own_rows, sums, sem,
):
    slots, rows = clear.shape
    total = ranks_ref.shape[0]
    places, flops, runouts = boards_ref.shape
    start = lax.axis_index("hand") * rows
    turn = lax.rem(slots - start, slots)

    cards = cards_ref[...]
    own_cards = pltpu.roll(cards, turn, 1)[:, :rows]
    card = lax.broadcasted_iota(jnp.int32, (CARDS, slots), 0)
    holders = jnp.where((card == cards[0:1]) | (card == cards[1:2]), 1.0, 0.0).astype(EXACT)
    card = lax.broadcasted_iota(jnp.int32, (CARDS, rows), 0)
    own_holders = (card == own_cards[0:1]) | (card == own_cards[1:2])
    own_holders = jnp.where(own_holders, 1.0, 0.0).astype(EXACT)

    boards = jnp.concatenate([boards_ref[place] for place in range(places)], axis=1)
    row = lax.broadcasted_iota(jnp.int32, (total, flops), 0)
    of_flop = row // runouts == lax.broadcasted_iota(jnp.int32, (total, flops), 1)
    spread = jnp.dot(
        jnp.where(of_flop, 1.0, 0.0).astype(jnp.bfloat16),
        boards.astype(jnp.float32).astype(jnp.bfloat16),
        preferred_element_type=jnp.float32,
    )
    row = lax.broadcasted_iota(jnp.int32, spread.shape, 0)
    lane = lax.broadcasted_iota(jnp.int32, spread.shape, 1)
    mine = lax.rem(row, runouts) == lax.rem(lane, runouts)
    card = lax.broadcasted_iota(jnp.int32, (total, CARDS), 1)
    on_board = card == DEAD_CARD
    for place in range(places):
        here = mine & (lane // runouts == place)
        found = jnp.sum(jnp.where(here, spread, 0.0), axis=1, keepdims=True)
        on_board = on_board | (card.astype(jnp.float32) == found)
    on_board = jnp.where(on_board, 1.0, 0.0).astype(EXACT)

    hits = jnp.dot(on_board, holders, preferred_element_type=jnp.float32)
    ranks = jnp.where(hits > 0.0, NO_RANK, ranks_ref[...].astype(jnp.float32))
    rank_rows[...] = ranks
    own_ranks = pltpu.roll(ranks, turn, 1)[:, :rows]
    own_rows[...] = own_ranks
    late_ranks[...] = ranks[total - late_ranks.shape[0] :]
    late_own[...] = own_ranks[total - late_own.shape[0] :]

    shared = lax.dot_general(holders, own_holders, TN, preferred_element_type=jnp.float32)
    clear[...] = jnp.maximum(1.0 - shared, 0.0).astype(jnp.bfloat16)

    act = act_ref[...]
    row = lax.broadcasted_iota(jnp.int32, (8, act.shape[1]), 0)
    weights = jnp.where(row == act, jnp.broadcast_to(pot_ref[...], row.shape), 0.0)
    weights_ref[...] = jnp.concatenate(split_bf16(weights), axis=0).astype(jnp.bfloat16)

    def copy(flop):
        return pltpu.make_async_copy(sums.at[flop], far_ref.at[flop], sem.at[flop])

    def sent(flop):
        @pl.when(flop < last)
        def _():
            copy(flop).start()

    last = sums.shape[0] - 1
    tables = (count_ref, rank_rows, own_rows, clear, holds, signs)
    add_flops(0, last + 1, *tables, sums, sent)
    near_ref[...] = sums[last]
    for flop in range(last):
        copy(flop).wait()


def showdown_scratch(runouts, slots, rows):
    return [
        pltpu.VMEM((runouts * RANKS, slots), EXACT),
        pltpu.VMEM((runouts * RANKS, rows), EXACT),
    ]


def first_flops(part, counts, ranks, boards, cards, pot, line_act, rows):
    total, slots = ranks.shape
    flops, lines = counts.shape[0], pot.shape[1]
    late = total // flops * (flops - part)
    return pl.pallas_call(
        first_kernel,
        out_shape=[
            jax.ShapeDtypeStruct((FAR_FLOPS, slots, rows), jnp.bfloat16),
            jax.ShapeDtypeStruct((slots, rows), jnp.bfloat16),
            jax.ShapeDtypeStruct((late, slots), jnp.float32),
            jax.ShapeDtypeStruct((late, rows), jnp.float32),
            jax.ShapeDtypeStruct((slots, rows), jnp.bfloat16),
            jax.ShapeDtypeStruct((8 * SPLITS, lines), jnp.bfloat16),
        ],
        in_specs=[SMEM] + [VMEM] * 5,
        out_specs=[ANY] + [VMEM] * 5,
        scratch_shapes=showdown_scratch(total // flops, slots, rows)
        + [
            pltpu.VMEM((total, slots), jnp.float32),
            pltpu.VMEM((total, rows), jnp.float32),
            pltpu.VMEM((part, slots, rows), jnp.bfloat16),
            pltpu.SemaphoreType.DMA((part - 1,)),
        ],
        name="first_flops",
        **params(FAR, 2 * 10**9, 10**7),
    )(counts, ranks, boards, cards, pot, line_act)


def other_kernel(
    part, count_ref, rank_rows, own_rows, clear, grouped_ref, far_ref, sums_ref,
    holds, signs, sem,
):
    copies = [
        pltpu.make_async_copy(far_ref.at[flop], sums_ref.at[flop], sem.at[flop])
        for flop in range(part - 1)
    ]
    for copy in copies:
        copy.start()
    tables = (count_ref, rank_rows, own_rows, clear, holds, signs)
    add_flops(part, count_ref.shape[0], *tables, sums_ref, lambda flop: None)
    for copy in copies:
        copy.wait()


def other_flops(part, counts, rank_rows, own_rows, clear, grouped, far):
    slots, rows = clear.shape
    flops = counts.shape[0]
    return pl.pallas_call(
        functools.partial(other_kernel, part),
        out_shape=jax.ShapeDtypeStruct((flops, slots, rows), jnp.bfloat16),
        in_specs=[SMEM, VMEM, VMEM, VMEM, ANY, ANY],
        out_specs=VMEM,
        scratch_shapes=showdown_scratch(rank_rows.shape[0] // (flops - part), slots, rows)
        + [pltpu.SemaphoreType.DMA((part - 1,))],
        name="other_flops",
        **params(FAR, 2 * 10**9, 10**7),
    )(counts, rank_rows, own_rows, clear, grouped, far)


def split_bf16(values):
    parts = []
    for _ in range(SPLITS):
        part = values.astype(jnp.bfloat16).astype(jnp.float32)
        parts.append(part)
        values = values - part
    return parts


def action_kernel(reach_ref, strategy_ref, weights_ref, out_ref):
    flops, rows, lines = strategy_ref.shape
    senders, per = reach_ref.shape
    own = rows // per
    reach = reach_ref[...]
    slot = lax.broadcasted_iota(jnp.int32, (senders, per), 0) * per + lax.broadcasted_iota(
        jnp.int32, (senders, per), 1
    )
    alive = jnp.where(slot < HANDS, reach, 0.0)
    total = jnp.sum(jnp.sum(alive, axis=1, keepdims=True), axis=0, keepdims=True)

    mine = reach_ref[pl.ds(pl.multiple_of(lax.axis_index("hand") * own, 8), own), :]
    mine = jnp.concatenate(split_bf16(mine), axis=0).astype(jnp.bfloat16)
    row = lax.broadcasted_iota(jnp.int32, (rows, own * SPLITS), 0)
    low = lax.rem(lax.broadcasted_iota(jnp.int32, (rows, own * SPLITS), 1), own) * per
    sender = jnp.where((row >= low) & (row < low + per), 1.0, 0.0).astype(jnp.bfloat16)
    wide = jnp.dot(sender, mine, preferred_element_type=jnp.float32)
    row = lax.broadcasted_iota(jnp.int32, (rows, per), 0)
    lane = lax.broadcasted_iota(jnp.int32, (rows, per), 1)
    own_reach = jnp.sum(jnp.where(lax.rem(row, per) == lane, wide, 0.0), axis=1, keepdims=True)
    scale = jnp.broadcast_to(own_reach / total, (rows, lines))

    weights = weights_ref[...]
    for flop in range(flops):
        line_reach = (strategy_ref[flop].astype(jnp.float32) * scale).astype(jnp.bfloat16)
        parts = lax.dot_general(weights, line_reach, NT, preferred_element_type=jnp.float32)
        sums = parts[0:8] + parts[8:16] + parts[16:24]
        out_ref[flop * GROUP : (flop + 1) * GROUP, :] = sums[0:GROUP]


def action_sums(reach, strategy, weights):
    flops, rows, lines = strategy.shape
    return pl.pallas_call(
        action_kernel,
        out_shape=jax.ShapeDtypeStruct((flops * GROUP, rows), jnp.float32),
        in_specs=[VMEM] * 3,
        out_specs=VMEM,
        name="action_sums",
        **params(4, 10**8),
    )(reach, strategy, weights)


def response_kernel(single, count_ref, weight_ref, sums_ref, near_ref, *refs):
    shards, out_ref = refs[:-1], refs[-1]
    flops, slots, rows = sums_ref.shape
    gathered = jnp.zeros((flops * GROUP, slots), jnp.float32)
    for step, shard in enumerate(shards):
        at = jnp.bitwise_xor(lax.axis_index("hand"), step) * rows
        empty = jnp.zeros((flops * GROUP, slots - rows), jnp.float32)
        gathered = gathered + pltpu.roll(jnp.concatenate([shard[...], empty], axis=1), at, 1)
    splits = split_bf16(gathered)
    values = jnp.zeros((1, rows), jnp.float32)
    weight_sum = 0
    for flop in range(flops):
        matrix = near_ref if flop == single else sums_ref.at[flop]
        low = flop * GROUP // 8 * 8
        left = jnp.concatenate([part[low : low + 8] for part in splits], axis=0)
        parts = jnp.dot(
            left.astype(jnp.bfloat16), matrix[...], preferred_element_type=jnp.float32
        )
        group = parts[0:8] + parts[8:16] + parts[16:24]
        at = flop * GROUP - low
        best = jnp.max(group[at : at + ACTS], axis=0, keepdims=True)
        weight = weight_ref[flop]
        count = jnp.full((1, rows), count_ref[flop].astype(jnp.float32))
        values = values + best * weight.astype(jnp.float32) / count
        weight_sum = weight_sum + weight
    tail = jnp.full((1, out_ref.shape[1] - rows), weight_sum.astype(jnp.float32))
    out_ref[...] = jnp.broadcast_to(jnp.concatenate([values, tail], axis=1), out_ref.shape)


def best_response(single, counts, weights, sums, near, shards, copies):
    rows = sums.shape[2]
    width = -(-(rows + 1) // 128) * 128
    return pl.pallas_call(
        functools.partial(response_kernel, single),
        out_shape=jax.ShapeDtypeStruct((copies, width), jnp.float32),
        in_specs=[SMEM, SMEM] + [VMEM] * (2 + len(shards)),
        out_specs=VMEM,
        name="best_response",
        **params(12, 10**9, 10**7),
    )(counts, weights, sums, near, *shards)


def finish_kernel(parts_ref, out_ref):
    rows = out_ref.shape[0]
    whole = jnp.sum(parts_ref[...], axis=0)
    weight = whole[rows : rows + 1]
    out_ref[...] = whole[:rows] / weight


def finish(parts, rows):
    return pl.pallas_call(
        finish_kernel,
        out_shape=jax.ShapeDtypeStruct((rows,), jnp.float32),
        in_specs=[VMEM],
        out_specs=VMEM,
        name="finish",
        **params(2),
    )(parts)


def body(boards_n, hands_n, reach_pre, strategy, ranks, boards, river_live, iso_weight, pot, line_act):
    lines, rows = strategy.shape[1:]
    flops, runouts, slots = ranks.shape
    part = PART

    send = reach_copies(boards_n * hands_n, reach_pre)
    reach = lax.all_to_all(send, ("board", "hand"), 0, 0, tiled=True)
    far, near, *tables, weights = first_flops(
        part,
        river_live,
        ranks.reshape(flops * runouts, slots),
        jnp.transpose(boards, (2, 0, 1)),
        hand_cards(),
        pot.reshape(1, lines),
        line_act.reshape(1, lines),
        rows,
    )

    grouped = action_sums(reach, jnp.swapaxes(strategy, 1, 2), weights)
    shards = [grouped]
    for step in range(1, hands_n):
        swap = [(source, source ^ step) for source in range(hands_n)]
        shards.append(lax.ppermute(grouped, "hand", swap))
    sums = other_flops(part, river_live, *tables, grouped, far)

    partial = best_response(part - 1, river_live, iso_weight, sums, near, shards, boards_n)
    return finish(lax.all_to_all(partial, "board", 0, 0, tiled=True), rows)


def solution(mesh):
    in_specs = (
        P(("board", "hand")),
        P("board", None, "hand"),
        P("board", None, None),
        P("board", None, None),
        P("board"),
        P("board"),
        P(),
        P(),
    )
    run = functools.partial(body, mesh.shape["board"], mesh.shape["hand"])
    return jax.shard_map(run, mesh=mesh, in_specs=in_specs, out_specs=P("hand"), check_vma=False)
```

```python
import functools

import jax
import jax.numpy as jnp
import numpy as np
from jax import lax
from jax.experimental import pallas as pl
from jax.experimental.pallas import tpu as pltpu
from jax.sharding import PartitionSpec as P

HANDS = 1326
HPAD = 1408
ACTS = 3
CARDS = 64
DEAD_CARD = 52
GROUP = 4
SPLITS = 3
PART = 4
FAR = 40
FAR_FLOPS = 24
RANKS = 128
USED_RANKS = 96
NO_RANK = 127.0

VMEM = pl.BlockSpec(memory_space=pltpu.VMEM)
ANY = pl.BlockSpec(memory_space=pltpu.HBM)
NT = (((1,), (1,)), ((), ()))
TN = (((0,), (0,)), ((), ()))
EXACT = jnp.float8_e4m3fn


def hand_cards():
    first_card, second_card = np.triu_indices(52, 1)
    padding = HPAD - HANDS
    first_card = np.concatenate([first_card, np.full(padding, 52)])
    second_card = np.concatenate([second_card, np.full(padding, 53)])
    return jnp.asarray(np.stack([first_card, second_card]), jnp.int32)


def params(megabytes, flops=0, moved=10**6):
    return dict(
        compiler_params=pltpu.CompilerParams(vmem_limit_bytes=megabytes << 20),
        cost_estimate=pl.CostEstimate(flops=flops, bytes_accessed=moved, transcendentals=0),
    )


def copies_kernel(reach_ref, send_ref):
    send_ref[...] = jnp.broadcast_to(reach_ref[...], send_ref.shape)


def reach_copies(devices, reach):
    per = reach.shape[0]
    return pl.pallas_call(
        copies_kernel,
        out_shape=jax.ShapeDtypeStruct((devices, per), jnp.float32),
        in_specs=[VMEM],
        out_specs=VMEM,
        name="reach_copies",
        **params(1, 10**10, 10**8),
    )(reach.reshape(1, per))


def level(width):
    return lax.broadcasted_iota(jnp.int32, (USED_RANKS, width), 0).astype(jnp.float32)


def add_flops(first, last, counts, rank_rows, own_rows, clear, holds, signs, sums_ref, sent):
    slots, rows = clear.shape
    runouts = holds.shape[0] // RANKS
    for low in range(0, runouts * RANKS, RANKS):
        holds[low + USED_RANKS : low + RANKS, :] = jnp.zeros((RANKS - USED_RANKS, slots), EXACT)
        signs[low + USED_RANKS : low + RANKS, :] = jnp.zeros((RANKS - USED_RANKS, rows), EXACT)

    one, zero = jnp.ones((32, slots), EXACT), jnp.zeros((32, slots), EXACT)
    down = lax.broadcasted_iota(jnp.int32, one.shape, 0)

    def add_runout(at, low):
        span = pl.ds(pl.multiple_of(low, RANKS), USED_RANKS)
        rank = jnp.broadcast_to(rank_rows[pl.ds(at, 1), :].astype(jnp.int32), one.shape)
        rank = rank.astype(jnp.int8)
        for step in range(0, USED_RANKS, one.shape[0]):
            held = jnp.where(rank == (down + step).astype(jnp.int8), one, zero)
            holds[pl.ds(pl.multiple_of(low + step, one.shape[0]), one.shape[0]), :] = held
        rank = own_rows[pl.ds(at, 1), :]
        live = jnp.where(rank < NO_RANK, 1.0, 0.0)
        sign = jnp.minimum(jnp.maximum(rank - level(rows), -1.0), 1.0)
        signs[span, :] = (sign * live).astype(EXACT)

    def multiply(flop, depth):
        right = signs[:depth, :]
        for lane in range(0, slots, 256):
            part = slice(lane, min(lane + 256, slots))
            sign = lax.dot_general(holds[:depth, part], right, TN, preferred_element_type=jnp.float32)
            sums_ref[flop, part, :] = sign.astype(jnp.bfloat16) * clear[part, :]

    def one_flop(flop, carry):
        count = counts[flop]

        def one_runout(runout, carry):
            add_runout((flop - first) * runouts + runout, runout * RANKS)
            return carry

        lax.fori_loop(0, count, one_runout, 0)

        @pl.when((lax.rem(count, 2) == 1) & (count > 1))
        def _():
            span = pl.ds(pl.multiple_of(count * RANKS, RANKS), RANKS)
            holds[span, :] = jnp.zeros((RANKS, slots), EXACT)
            signs[span, :] = jnp.zeros((RANKS, rows), EXACT)

        @pl.when(count == 1)
        def _():
            multiply(flop, RANKS)

        for step in range(2, runouts + 1, 2):

            @pl.when((count == step) | ((count == step - 1) & (count > 1)))
            def _():
                multiply(flop, step * RANKS)

        sent(flop)
        return carry

    lax.fori_loop(first, last, one_flop, 0)


def first_kernel(
    count_ref, ranks_ref, boards_ref, cards_ref, pot_ref, act_ref,
    far_ref, near_ref, late_ranks, late_own, clear, weights_ref,
    counts, holds, signs, rank_rows, own_rows, sums, sem,
):
    read_counts(count_ref, counts)
    slots, rows = clear.shape
    total = ranks_ref.shape[0]
    places, flops, runouts = boards_ref.shape
    start = lax.axis_index("hand") * rows
    turn = lax.rem(slots - start, slots)

    cards = cards_ref[...]
    own_cards = pltpu.roll(cards, turn, 1)[:, :rows]
    card = lax.broadcasted_iota(jnp.int32, (CARDS, slots), 0)
    holders = jnp.where((card == cards[0:1]) | (card == cards[1:2]), 1.0, 0.0).astype(EXACT)
    card = lax.broadcasted_iota(jnp.int32, (CARDS, rows), 0)
    own_holders = (card == own_cards[0:1]) | (card == own_cards[1:2])
    own_holders = jnp.where(own_holders, 1.0, 0.0).astype(EXACT)

    boards = jnp.concatenate([boards_ref[place] for place in range(places)], axis=1)
    row = lax.broadcasted_iota(jnp.int32, (total, flops), 0)
    of_flop = row // runouts == lax.broadcasted_iota(jnp.int32, (total, flops), 1)
    spread = jnp.dot(
        jnp.where(of_flop, 1.0, 0.0).astype(jnp.bfloat16),
        boards.astype(jnp.float32).astype(jnp.bfloat16),
        preferred_element_type=jnp.float32,
    )
    row = lax.broadcasted_iota(jnp.int32, spread.shape, 0)
    lane = lax.broadcasted_iota(jnp.int32, spread.shape, 1)
    mine = lax.rem(row, runouts) == lax.rem(lane, runouts)
    card = lax.broadcasted_iota(jnp.int32, (total, CARDS), 1)
    on_board = card == DEAD_CARD
    for place in range(places):
        here = mine & (lane // runouts == place)
        found = jnp.sum(jnp.where(here, spread, 0.0), axis=1, keepdims=True)
        on_board = on_board | (card.astype(jnp.float32) == found)
    on_board = jnp.where(on_board, 1.0, 0.0).astype(EXACT)

    hits = jnp.dot(on_board, holders, preferred_element_type=jnp.float32)
    ranks = jnp.where(hits > 0.0, NO_RANK, ranks_ref[...].astype(jnp.float32))
    rank_rows[...] = ranks
    own_ranks = pltpu.roll(ranks, turn, 1)[:, :rows]
    own_rows[...] = own_ranks
    late_ranks[...] = ranks[total - late_ranks.shape[0] :]
    late_own[...] = own_ranks[total - late_own.shape[0] :]

    shared = lax.dot_general(holders, own_holders, TN, preferred_element_type=jnp.float32)
    clear[...] = jnp.maximum(1.0 - shared, 0.0).astype(jnp.bfloat16)

    act = act_ref[...]
    row = lax.broadcasted_iota(jnp.int32, (8, act.shape[1]), 0)
    weights = jnp.where(row == act, jnp.broadcast_to(pot_ref[...], row.shape), 0.0)
    weights_ref[...] = jnp.concatenate(split_bf16(weights), axis=0).astype(jnp.bfloat16)

    def copy(flop):
        return pltpu.make_async_copy(sums.at[flop], far_ref.at[flop], sem.at[flop])

    def sent(flop):
        @pl.when(flop < last)
        def _():
            copy(flop).start()

    last = sums.shape[0] - 1
    tables = (counts, rank_rows, own_rows, clear, holds, signs)
    add_flops(0, last + 1, *tables, sums, sent)
    near_ref[...] = sums[last]
    for flop in range(last):
        copy(flop).wait()


def read_counts(count_ref, counts):
    for flop in range(count_ref.shape[1]):
        counts[flop] = count_ref[0, flop]


def showdown_scratch(flops, runouts, slots, rows):
    return [
        pltpu.SMEM((flops,), jnp.int32),
        pltpu.VMEM((runouts * RANKS, slots), EXACT),
        pltpu.VMEM((runouts * RANKS, rows), EXACT),
    ]


def first_flops(part, counts, ranks, boards, cards, pot, line_act, rows):
    total, slots = ranks.shape
    flops, lines = counts.shape[1], pot.shape[1]
    late = total // flops * (flops - part)
    return pl.pallas_call(
        first_kernel,
        out_shape=[
            jax.ShapeDtypeStruct((FAR_FLOPS, slots, rows), jnp.bfloat16),
            jax.ShapeDtypeStruct((slots, rows), jnp.bfloat16),
            jax.ShapeDtypeStruct((late, slots), jnp.float32),
            jax.ShapeDtypeStruct((late, rows), jnp.float32),
            jax.ShapeDtypeStruct((slots, rows), jnp.bfloat16),
            jax.ShapeDtypeStruct((8 * SPLITS, lines), jnp.bfloat16),
        ],
        in_specs=[VMEM] * 6,
        out_specs=[ANY] + [VMEM] * 5,
        scratch_shapes=showdown_scratch(flops, total // flops, slots, rows)
        + [
            pltpu.VMEM((total, slots), jnp.float32),
            pltpu.VMEM((total, rows), jnp.float32),
            pltpu.VMEM((part, slots, rows), jnp.bfloat16),
            pltpu.SemaphoreType.DMA((part - 1,)),
        ],
        name="first_flops",
        **params(FAR, 2 * 10**9, 10**7),
    )(counts, ranks, boards, cards, pot, line_act)


def other_kernel(
    part, count_ref, rank_rows, own_rows, clear, grouped_ref, far_ref, sums_ref,
    counts, holds, signs, sem,
):
    read_counts(count_ref, counts)
    copies = [
        pltpu.make_async_copy(far_ref.at[flop], sums_ref.at[flop], sem.at[flop])
        for flop in range(part - 1)
    ]
    for copy in copies:
        copy.start()
    tables = (counts, rank_rows, own_rows, clear, holds, signs)
    add_flops(part, count_ref.shape[1], *tables, sums_ref, lambda flop: None)
    for copy in copies:
        copy.wait()


def other_flops(part, counts, rank_rows, own_rows, clear, grouped, far):
    slots, rows = clear.shape
    flops = counts.shape[1]
    return pl.pallas_call(
        functools.partial(other_kernel, part),
        out_shape=jax.ShapeDtypeStruct((flops, slots, rows), jnp.bfloat16),
        in_specs=[VMEM] * 4 + [ANY] * 2,
        out_specs=VMEM,
        scratch_shapes=showdown_scratch(flops, rank_rows.shape[0] // (flops - part), slots, rows)
        + [pltpu.SemaphoreType.DMA((part - 1,))],
        name="other_flops",
        **params(FAR, 2 * 10**9, 10**7),
    )(counts, rank_rows, own_rows, clear, grouped, far)


def split_bf16(values):
    parts = []
    for _ in range(SPLITS):
        part = values.astype(jnp.bfloat16).astype(jnp.float32)
        parts.append(part)
        values = values - part
    return parts


def action_kernel(reach_ref, strategy_ref, weights_ref, out_ref):
    flops, rows, lines = strategy_ref.shape
    senders, per = reach_ref.shape
    own = rows // per
    reach = reach_ref[...]
    slot = lax.broadcasted_iota(jnp.int32, (senders, per), 0) * per + lax.broadcasted_iota(
        jnp.int32, (senders, per), 1
    )
    alive = jnp.where(slot < HANDS, reach, 0.0)
    total = jnp.sum(jnp.sum(alive, axis=1, keepdims=True), axis=0, keepdims=True)

    mine = reach_ref[pl.ds(pl.multiple_of(lax.axis_index("hand") * own, 8), own), :]
    mine = jnp.concatenate(split_bf16(mine), axis=0).astype(jnp.bfloat16)
    row = lax.broadcasted_iota(jnp.int32, (rows, own * SPLITS), 0)
    low = lax.rem(lax.broadcasted_iota(jnp.int32, (rows, own * SPLITS), 1), own) * per
    sender = jnp.where((row >= low) & (row < low + per), 1.0, 0.0).astype(jnp.bfloat16)
    wide = jnp.dot(sender, mine, preferred_element_type=jnp.float32)
    row = lax.broadcasted_iota(jnp.int32, (rows, per), 0)
    lane = lax.broadcasted_iota(jnp.int32, (rows, per), 1)
    own_reach = jnp.sum(jnp.where(lax.rem(row, per) == lane, wide, 0.0), axis=1, keepdims=True)
    scale = jnp.broadcast_to(own_reach / total, (rows, lines))

    weights = weights_ref[...]
    for flop in range(flops):
        line_reach = (strategy_ref[flop].astype(jnp.float32) * scale).astype(jnp.bfloat16)
        parts = lax.dot_general(weights, line_reach, NT, preferred_element_type=jnp.float32)
        sums = parts[0:8] + parts[8:16] + parts[16:24]
        out_ref[flop * GROUP : (flop + 1) * GROUP, :] = sums[0:GROUP]


def action_sums(reach, strategy, weights):
    flops, rows, lines = strategy.shape
    return pl.pallas_call(
        action_kernel,
        out_shape=jax.ShapeDtypeStruct((flops * GROUP, rows), jnp.float32),
        in_specs=[VMEM] * 3,
        out_specs=VMEM,
        name="action_sums",
        **params(4, 10**8),
    )(reach, strategy, weights)


def response_kernel(single, count_ref, weight_ref, sums_ref, near_ref, *refs):
    shards, out_ref, products = refs[:-2], refs[-2], refs[-1]
    flops, slots, rows = sums_ref.shape
    gathered = jnp.zeros((flops * GROUP, slots), jnp.float32)
    for step, shard in enumerate(shards):
        at = jnp.bitwise_xor(lax.axis_index("hand"), step) * rows
        empty = jnp.zeros((flops * GROUP, slots - rows), jnp.float32)
        gathered = gathered + pltpu.roll(jnp.concatenate([shard[...], empty], axis=1), at, 1)
    splits = split_bf16(gathered)
    for flop in range(flops):
        matrix = near_ref if flop == single else sums_ref.at[flop]
        low = flop * GROUP // 8 * 8
        left = jnp.concatenate([part[low : low + 8] for part in splits], axis=0)
        products[flop] = jnp.dot(
            left.astype(jnp.bfloat16), matrix[...], preferred_element_type=jnp.float32
        )

    values = jnp.zeros((1, rows), jnp.float32)
    weights = weight_ref[...].astype(jnp.float32)
    counts = count_ref[...].astype(jnp.float32)
    for flop in range(flops):
        group = products[flop, 0:8] + products[flop, 8:16] + products[flop, 16:24]
        at = flop * GROUP % 8
        best = jnp.max(group[at : at + ACTS], axis=0, keepdims=True)
        values = values + best * weights[:, flop : flop + 1] / counts[:, flop : flop + 1]
    tail = jnp.sum(weights, axis=1, keepdims=True)
    tail = jnp.broadcast_to(tail, (1, out_ref.shape[1] - rows))
    out_ref[...] = jnp.broadcast_to(jnp.concatenate([values, tail], axis=1), out_ref.shape)


def best_response(single, counts, weights, sums, near, shards, copies):
    rows = sums.shape[2]
    width = -(-(rows + 1) // 128) * 128
    return pl.pallas_call(
        functools.partial(response_kernel, single),
        out_shape=jax.ShapeDtypeStruct((copies, width), jnp.float32),
        in_specs=[VMEM] * (4 + len(shards)),
        out_specs=VMEM,
        scratch_shapes=[pltpu.VMEM((sums.shape[0], 8 * SPLITS, rows), jnp.float32)],
        name="best_response",
        **params(12, 10**9, 10**7),
    )(counts, weights, sums, near, *shards)


def finish_kernel(parts_ref, out_ref):
    rows = out_ref.shape[0]
    whole = jnp.sum(parts_ref[...], axis=0)
    weight = whole[rows : rows + 1]
    out_ref[...] = whole[:rows] / weight


def finish(parts, rows):
    return pl.pallas_call(
        finish_kernel,
        out_shape=jax.ShapeDtypeStruct((rows,), jnp.float32),
        in_specs=[VMEM],
        out_specs=VMEM,
        name="finish",
        **params(2),
    )(parts)


def body(boards_n, hands_n, reach_pre, strategy, ranks, boards, river_live, iso_weight, pot, line_act):
    lines, rows = strategy.shape[1:]
    flops, runouts, slots = ranks.shape
    part = PART
    counts = river_live.reshape(1, flops)

    send = reach_copies(boards_n * hands_n, reach_pre)
    reach = lax.all_to_all(send, ("board", "hand"), 0, 0, tiled=True)
    far, near, *tables, weights = first_flops(
        part,
        counts,
        ranks.reshape(flops * runouts, slots),
        jnp.transpose(boards, (2, 0, 1)),
        hand_cards(),
        pot.reshape(1, lines),
        line_act.reshape(1, lines),
        rows,
    )

    grouped = action_sums(reach, jnp.swapaxes(strategy, 1, 2), weights)
    shards = [grouped]
    for step in range(1, hands_n):
        swap = [(source, source ^ step) for source in range(hands_n)]
        shards.append(lax.ppermute(grouped, "hand", swap))
    sums = other_flops(part, counts, *tables, grouped, far)

    weights = iso_weight.reshape(1, flops)
    partial = best_response(part - 1, counts, weights, sums, near, shards, boards_n)
    return finish(lax.all_to_all(partial, "board", 0, 0, tiled=True), rows)


def solution(mesh):
    in_specs = (
        P(("board", "hand")),
        P("board", None, "hand"),
        P("board", None, None),
        P("board", None, None),
        P("board"),
        P("board"),
        P(),
        P(),
    )
    run = functools.partial(body, mesh.shape["board"], mesh.shape["hand"])
    return jax.shard_map(run, mesh=mesh, in_specs=in_specs, out_specs=P("hand"), check_vma=False)
```

```python
import functools

import jax
import jax.numpy as jnp
import numpy as np
from jax import lax
from jax.experimental import pallas as pl
from jax.experimental.pallas import tpu as pltpu
from jax.sharding import PartitionSpec as P

HANDS = 1326
HPAD = 1408
ACTS = 3
CARDS = 64
DEAD_CARD = 52
SPLITS = 3
PART = 4
FAR = 40
FAR_FLOPS = 24
RANKS = 128
FEW = 8
USED_RANKS = 96
NO_RANK = 127.0

VMEM = pl.BlockSpec(memory_space=pltpu.VMEM)
ANY = pl.BlockSpec(memory_space=pltpu.HBM)
NT = (((1,), (1,)), ((), ()))
TN = (((0,), (0,)), ((), ()))
EXACT = jnp.float8_e4m3fn


def hand_cards():
    first_card, second_card = np.triu_indices(52, 1)
    padding = HPAD - HANDS
    first_card = np.concatenate([first_card, np.full(padding, 52)])
    second_card = np.concatenate([second_card, np.full(padding, 53)])
    return jnp.asarray(np.stack([first_card, second_card]), jnp.int32)


def params(megabytes, flops=0, moved=10**6):
    return dict(
        compiler_params=pltpu.CompilerParams(vmem_limit_bytes=megabytes << 20),
        cost_estimate=pl.CostEstimate(flops=flops, bytes_accessed=moved, transcendentals=0),
    )


def copies_kernel(reach_ref, send_ref):
    send_ref[...] = jnp.broadcast_to(reach_ref[...], send_ref.shape)


def reach_copies(devices, reach):
    per = reach.shape[0]
    return pl.pallas_call(
        copies_kernel,
        out_shape=jax.ShapeDtypeStruct((devices, per), jnp.float32),
        in_specs=[VMEM],
        out_specs=VMEM,
        name="reach_copies",
        **params(1, 10**10, 10**8),
    )(reach.reshape(1, per))


def level(width):
    return lax.broadcasted_iota(jnp.int32, (USED_RANKS, width), 0).astype(jnp.float32)


def slot_parts(slots):
    return [slice(low, min(low + 256, slots)) for low in range(0, slots, 256)]


def add_flops(first, last, rows_from, counts, rank_rows, own_rows, clear, holds, signs, place, sent):
    slots, rows = clear.shape
    runouts = holds.shape[0] // RANKS
    for low in range(0, runouts * RANKS, RANKS):
        holds[low + USED_RANKS : low + RANKS, :] = jnp.zeros((RANKS - USED_RANKS, slots), EXACT)
        signs[low + USED_RANKS : low + RANKS, :] = jnp.zeros((RANKS - USED_RANKS, rows), EXACT)

    parts = slot_parts(slots)
    tile = 32

    def hold(rank, low, part):
        shape = (tile, part.stop - part.start)
        rank = jnp.broadcast_to(rank[:, part].astype(jnp.int32), shape)
        rank = rank.astype(jnp.int8)
        down = lax.broadcasted_iota(jnp.int32, shape, 0)
        one, zero = jnp.ones(shape, EXACT), jnp.zeros(shape, EXACT)
        for step in range(0, USED_RANKS, tile):
            held = jnp.where(rank == (down + step).astype(jnp.int8), one, zero)
            holds[pl.ds(low + step, tile), part] = held

    def sign(at, low):
        rank = own_rows[pl.ds(at, 1), :]
        live = jnp.where(rank < NO_RANK, 1.0, 0.0)
        against = jnp.minimum(jnp.maximum(rank - level(rows), -1.0), 1.0)
        signs[pl.ds(low, USED_RANKS), :] = (against * live).astype(EXACT)

    def multiply(flop, depth, part):
        product = lax.dot_general(
            holds[:depth, part], signs[:depth, :], TN, preferred_element_type=jnp.float32
        )
        target, index = place(flop, part)
        target[index] = product.astype(jnp.bfloat16) * clear[part, :]

    def one_flop(flop, carry):
        count = counts[flop]
        row = (flop - rows_from) * runouts

        for few in range(1, FEW + 1):

            @pl.when(count == few)
            def _():
                for runout in range(few):
                    sign(row + runout, runout * RANKS)
                ranks = [rank_rows[pl.ds(row + runout, 1), :] for runout in range(few)]
                for chunk, part in enumerate(parts):
                    for runout, rank in enumerate(ranks):
                        hold(rank, runout * RANKS, part)
                    multiply(flop, few * RANKS, part)
                    sent(flop, chunk, part)

        @pl.when(count > FEW)
        def _():
            def one_runout(runout, carry):
                low = pl.multiple_of(runout * RANKS, RANKS)
                hold(rank_rows[pl.ds(row + runout, 1), :], low, slice(0, slots))
                sign(row + runout, low)
                return carry

            lax.fori_loop(0, count, one_runout, 0)

            @pl.when(lax.rem(count, 2) == 1)
            def _():
                span = pl.ds(pl.multiple_of(count * RANKS, RANKS), RANKS)
                holds[span, :] = jnp.zeros((RANKS, slots), EXACT)
                signs[span, :] = jnp.zeros((RANKS, rows), EXACT)

        for step in range(FEW + 2, runouts + 1, 2):

            @pl.when((count == step) | (count == step - 1))
            def _():
                for chunk, part in enumerate(parts):
                    multiply(flop, step * RANKS, part)
                    sent(flop, chunk, part)

        return carry

    lax.fori_loop(first, last, one_flop, 0)


def first_kernel(
    count_ref, ranks_ref, boards_ref, cards_ref, pot_ref, act_ref,
    far_ref, near_ref, late_ranks, late_own, clear, weights_ref,
    counts, holds, signs, rank_rows, own_rows, sums, sem,
):
    read_counts(count_ref, counts)
    slots, rows = clear.shape
    total = ranks_ref.shape[0]
    places, flops, runouts = boards_ref.shape
    start = lax.axis_index("hand") * rows
    turn = lax.rem(slots - start, slots)

    cards = cards_ref[...]
    own_cards = pltpu.roll(cards, turn, 1)[:, :rows]
    card = lax.broadcasted_iota(jnp.int32, (CARDS, slots), 0)
    holders = jnp.where((card == cards[0:1]) | (card == cards[1:2]), 1.0, 0.0).astype(EXACT)
    card = lax.broadcasted_iota(jnp.int32, (CARDS, rows), 0)
    own_holders = (card == own_cards[0:1]) | (card == own_cards[1:2])
    own_holders = jnp.where(own_holders, 1.0, 0.0).astype(EXACT)

    boards = jnp.concatenate([boards_ref[place] for place in range(places)], axis=1)
    row = lax.broadcasted_iota(jnp.int32, (total, flops), 0)
    of_flop = row // runouts == lax.broadcasted_iota(jnp.int32, (total, flops), 1)
    spread = jnp.dot(
        jnp.where(of_flop, 1.0, 0.0).astype(jnp.bfloat16),
        boards.astype(jnp.float32).astype(jnp.bfloat16),
        preferred_element_type=jnp.float32,
    )
    row = lax.broadcasted_iota(jnp.int32, spread.shape, 0)
    lane = lax.broadcasted_iota(jnp.int32, spread.shape, 1)
    mine = lax.rem(row, runouts) == lax.rem(lane, runouts)
    card = lax.broadcasted_iota(jnp.int32, (total, CARDS), 1)
    on_board = card == DEAD_CARD
    for place in range(places):
        here = mine & (lane // runouts == place)
        found = jnp.sum(jnp.where(here, spread, 0.0), axis=1, keepdims=True)
        on_board = on_board | (card.astype(jnp.float32) == found)
    on_board = jnp.where(on_board, 1.0, 0.0).astype(EXACT)

    hits = jnp.dot(on_board, holders, preferred_element_type=jnp.float32)
    ranks = jnp.where(hits > 0.0, NO_RANK, ranks_ref[...].astype(jnp.float32))
    rank_rows[...] = ranks
    own_ranks = pltpu.roll(ranks, turn, 1)[:, :rows]
    own_rows[...] = own_ranks
    late_ranks[...] = ranks[total - late_ranks.shape[0] :]
    late_own[...] = own_ranks[total - late_own.shape[0] :]

    shared = lax.dot_general(holders, own_holders, TN, preferred_element_type=jnp.float32)
    clear[...] = jnp.maximum(1.0 - shared, 0.0).astype(jnp.bfloat16)

    act = act_ref[...]
    row = lax.broadcasted_iota(jnp.int32, (8, act.shape[1]), 0)
    weights = jnp.where(row == act, jnp.broadcast_to(pot_ref[...], row.shape), 0.0)
    weights_ref[...] = jnp.concatenate(split_bf16(weights), axis=0).astype(jnp.bfloat16)

    def copy(flop, chunk, part):
        span = pl.ds(part.start, part.stop - part.start)
        return pltpu.make_async_copy(
            sums.at[flop, span], far_ref.at[flop, span], sem.at[flop, chunk]
        )

    last = sums.shape[0]
    tables = (counts, rank_rows, own_rows, clear, holds, signs)
    add_flops(
        0, last, 0, *tables,
        lambda flop, part: (sums, (flop, part)),
        lambda flop, chunk, part: copy(flop, chunk, part).start(),
    )
    add_flops(
        last, last + 1, 0, *tables, lambda flop, part: (near_ref, part), lambda *done: None
    )
    for flop in range(last):
        for chunk, part in enumerate(slot_parts(slots)):
            copy(flop, chunk, part).wait()


def read_counts(count_ref, counts):
    for flop in range(count_ref.shape[1]):
        counts[flop] = count_ref[0, flop]


def showdown_scratch(flops, runouts, slots, rows):
    return [
        pltpu.SMEM((flops,), jnp.int32),
        pltpu.VMEM((runouts * RANKS, slots), EXACT),
        pltpu.VMEM((runouts * RANKS, rows), EXACT),
    ]


def first_flops(part, counts, ranks, boards, cards, pot, line_act, rows):
    total, slots = ranks.shape
    flops, lines = counts.shape[1], pot.shape[1]
    late = total // flops * (flops - part)
    return pl.pallas_call(
        first_kernel,
        out_shape=[
            jax.ShapeDtypeStruct((FAR_FLOPS, slots, rows), jnp.bfloat16),
            jax.ShapeDtypeStruct((slots, rows), jnp.bfloat16),
            jax.ShapeDtypeStruct((late, slots), jnp.float32),
            jax.ShapeDtypeStruct((late, rows), jnp.float32),
            jax.ShapeDtypeStruct((slots, rows), jnp.bfloat16),
            jax.ShapeDtypeStruct((8 * SPLITS, lines), jnp.bfloat16),
        ],
        in_specs=[VMEM] * 6,
        out_specs=[ANY] + [VMEM] * 5,
        scratch_shapes=showdown_scratch(flops, total // flops, slots, rows)
        + [
            pltpu.VMEM((total, slots), jnp.float32),
            pltpu.VMEM((total, rows), jnp.float32),
            pltpu.VMEM((part - 1, slots, rows), jnp.bfloat16),
            pltpu.SemaphoreType.DMA((part - 1, len(slot_parts(slots)))),
        ],
        name="first_flops",
        **params(FAR, 2 * 10**9, 10**7),
    )(counts, ranks, boards, cards, pot, line_act)


def other_kernel(
    part, count_ref, rank_rows, own_rows, clear, grouped_ref, far_ref, sums_ref,
    counts, holds, signs, sem,
):
    read_counts(count_ref, counts)
    copies = [
        pltpu.make_async_copy(far_ref.at[flop], sums_ref.at[flop], sem.at[flop])
        for flop in range(part - 1)
    ]
    for copy in copies:
        copy.start()
    tables = (counts, rank_rows, own_rows, clear, holds, signs)
    add_flops(
        part, count_ref.shape[1], part, *tables,
        lambda flop, part: (sums_ref, (flop, part)),
        lambda *done: None,
    )
    for copy in copies:
        copy.wait()


def other_flops(part, counts, rank_rows, own_rows, clear, grouped, far):
    slots, rows = clear.shape
    flops = counts.shape[1]
    return pl.pallas_call(
        functools.partial(other_kernel, part),
        out_shape=jax.ShapeDtypeStruct((flops, slots, rows), jnp.bfloat16),
        in_specs=[VMEM] * 4 + [ANY] * 2,
        out_specs=VMEM,
        scratch_shapes=showdown_scratch(flops, rank_rows.shape[0] // (flops - part), slots, rows)
        + [pltpu.SemaphoreType.DMA((part - 1,))],
        name="other_flops",
        **params(FAR, 2 * 10**9, 10**7),
    )(counts, rank_rows, own_rows, clear, grouped, far)


def split_bf16(values):
    parts = []
    for _ in range(SPLITS):
        part = values.astype(jnp.bfloat16).astype(jnp.float32)
        parts.append(part)
        values = values - part
    return parts


def action_kernel(reach_ref, strategy_ref, weights_ref, out_ref):
    flops, rows, lines = strategy_ref.shape
    senders, per = reach_ref.shape
    own = rows // per
    reach = reach_ref[...]
    slot = lax.broadcasted_iota(jnp.int32, (senders, per), 0) * per + lax.broadcasted_iota(
        jnp.int32, (senders, per), 1
    )
    alive = jnp.where(slot < HANDS, reach, 0.0)
    total = jnp.sum(jnp.sum(alive, axis=1, keepdims=True), axis=0, keepdims=True)

    mine = reach_ref[pl.ds(pl.multiple_of(lax.axis_index("hand") * own, 8), own), :]
    mine = jnp.concatenate(split_bf16(mine), axis=0).astype(jnp.bfloat16)
    row = lax.broadcasted_iota(jnp.int32, (rows, own * SPLITS), 0)
    low = lax.rem(lax.broadcasted_iota(jnp.int32, (rows, own * SPLITS), 1), own) * per
    sender = jnp.where((row >= low) & (row < low + per), 1.0, 0.0).astype(jnp.bfloat16)
    wide = jnp.dot(sender, mine, preferred_element_type=jnp.float32)
    row = lax.broadcasted_iota(jnp.int32, (rows, per), 0)
    lane = lax.broadcasted_iota(jnp.int32, (rows, per), 1)
    own_reach = jnp.sum(jnp.where(lax.rem(row, per) == lane, wide, 0.0), axis=1, keepdims=True)
    scale = jnp.broadcast_to(own_reach / total, (rows, lines))

    weights = weights_ref[...]
    for flop in range(flops):
        line_reach = (strategy_ref[flop].astype(jnp.float32) * scale).astype(jnp.bfloat16)
        parts = lax.dot_general(weights, line_reach, NT, preferred_element_type=jnp.float32)
        sums = parts[0:8] + parts[8:16] + parts[16:24]
        out_ref[flop * ACTS : (flop + 1) * ACTS, :] = sums[0:ACTS]


def action_sums(reach, strategy, weights):
    flops, rows, lines = strategy.shape
    return pl.pallas_call(
        action_kernel,
        out_shape=jax.ShapeDtypeStruct((flops * ACTS, rows), jnp.float32),
        in_specs=[VMEM] * 3,
        out_specs=VMEM,
        name="action_sums",
        **params(4, 10**8),
    )(reach, strategy, weights)


def row_span(flop):
    low = flop * ACTS // 8 * 8
    return low, (flop * ACTS + ACTS + 7) // 8 * 8


def response_kernel(single, count_ref, weight_ref, sums_ref, near_ref, *refs):
    shards, out_ref, products = refs[:-2], refs[-2], refs[-1]
    flops, slots, rows = sums_ref.shape
    gathered = jnp.zeros((flops * ACTS, slots), jnp.float32)
    for step, shard in enumerate(shards):
        at = jnp.bitwise_xor(lax.axis_index("hand"), step) * rows
        empty = jnp.zeros((flops * ACTS, slots - rows), jnp.float32)
        gathered = gathered + pltpu.roll(jnp.concatenate([shard[...], empty], axis=1), at, 1)
    splits = split_bf16(gathered)
    for flop in range(flops):
        matrix = near_ref if flop == single else sums_ref.at[flop]
        low, high = row_span(flop)
        left = jnp.concatenate([part[low:high] for part in splits], axis=0)
        products[flop, : left.shape[0]] = jnp.dot(
            left.astype(jnp.bfloat16), matrix[...], preferred_element_type=jnp.float32
        )

    values = jnp.zeros((1, rows), jnp.float32)
    weights = weight_ref[...].astype(jnp.float32)
    counts = count_ref[...].astype(jnp.float32)
    for flop in range(flops):
        low, high = row_span(flop)
        size, at = high - low, flop * ACTS - low
        group = sum(products[flop, part * size : (part + 1) * size] for part in range(SPLITS))
        best = jnp.max(group[at : at + ACTS], axis=0, keepdims=True)
        values = values + best * weights[:, flop : flop + 1] / counts[:, flop : flop + 1]
    tail = jnp.sum(weights, axis=1, keepdims=True)
    tail = jnp.broadcast_to(tail, (1, out_ref.shape[1] - rows))
    out_ref[...] = jnp.broadcast_to(jnp.concatenate([values, tail], axis=1), out_ref.shape)


def best_response(single, counts, weights, sums, near, shards, copies):
    rows = sums.shape[2]
    width = -(-(rows + 1) // 128) * 128
    return pl.pallas_call(
        functools.partial(response_kernel, single),
        out_shape=jax.ShapeDtypeStruct((copies, width), jnp.float32),
        in_specs=[VMEM] * (4 + len(shards)),
        out_specs=VMEM,
        scratch_shapes=[pltpu.VMEM((sums.shape[0], 16 * SPLITS, rows), jnp.float32)],
        name="best_response",
        **params(12, 10**9, 10**7),
    )(counts, weights, sums, near, *shards)


def finish_kernel(parts_ref, out_ref):
    rows = out_ref.shape[0]
    whole = jnp.sum(parts_ref[...], axis=0)
    weight = whole[rows : rows + 1]
    out_ref[...] = whole[:rows] / weight


def finish(parts, rows):
    return pl.pallas_call(
        finish_kernel,
        out_shape=jax.ShapeDtypeStruct((rows,), jnp.float32),
        in_specs=[VMEM],
        out_specs=VMEM,
        name="finish",
        **params(2),
    )(parts)


def body(boards_n, hands_n, reach_pre, strategy, ranks, boards, river_live, iso_weight, pot, line_act):
    lines, rows = strategy.shape[1:]
    flops, runouts, slots = ranks.shape
    part = PART
    counts = river_live.reshape(1, flops)

    send = reach_copies(boards_n * hands_n, reach_pre)
    reach = lax.all_to_all(send, ("board", "hand"), 0, 0, tiled=True)
    far, near, *tables, weights = first_flops(
        part,
        counts,
        ranks.reshape(flops * runouts, slots),
        jnp.transpose(boards, (2, 0, 1)),
        hand_cards(),
        pot.reshape(1, lines),
        line_act.reshape(1, lines),
        rows,
    )

    grouped = action_sums(reach, jnp.swapaxes(strategy, 1, 2), weights)
    shards = [grouped]
    for step in range(1, hands_n):
        swap = [(source, source ^ step) for source in range(hands_n)]
        shards.append(lax.ppermute(grouped, "hand", swap))
    sums = other_flops(part, counts, *tables, grouped, far)

    weights = iso_weight.reshape(1, flops)
    partial = best_response(part - 1, counts, weights, sums, near, shards, boards_n)
    return finish(lax.all_to_all(partial, "board", 0, 0, tiled=True), rows)


def solution(mesh):
    in_specs = (
        P(("board", "hand")),
        P("board", None, "hand"),
        P("board", None, None),
        P("board", None, None),
        P("board"),
        P("board"),
        P(),
        P(),
    )
    run = functools.partial(body, mesh.shape["board"], mesh.shape["hand"])
    return jax.shard_map(run, mesh=mesh, in_specs=in_specs, out_specs=P("hand"), check_vma=False)
```

```python
import functools

import jax
import jax.numpy as jnp
import numpy as np
from jax import lax
from jax.experimental import pallas as pl
from jax.experimental.pallas import tpu as pltpu
from jax.sharding import PartitionSpec as P

HANDS = 1326
HPAD = 1408
ACTS = 3
CARDS = 64
DEAD_CARD = 52
SPLITS = 3
PART = 4
FAR = 40
FAR_FLOPS = 24
RANKS = 128
USED_RANKS = 96
NO_RANK = 127.0

VMEM = pl.BlockSpec(memory_space=pltpu.VMEM)
ANY = pl.BlockSpec(memory_space=pltpu.HBM)
NT = (((1,), (1,)), ((), ()))
TN = (((0,), (0,)), ((), ()))
EXACT = jnp.float8_e4m3fn


def hand_cards():
    first_card, second_card = np.triu_indices(52, 1)
    padding = HPAD - HANDS
    first_card = np.concatenate([first_card, np.full(padding, 52)])
    second_card = np.concatenate([second_card, np.full(padding, 53)])
    return jnp.asarray(np.stack([first_card, second_card]), jnp.int32)


def params(megabytes, flops=0, moved=10**6):
    return dict(
        compiler_params=pltpu.CompilerParams(vmem_limit_bytes=megabytes << 20),
        cost_estimate=pl.CostEstimate(flops=flops, bytes_accessed=moved, transcendentals=0),
    )


def copies_kernel(reach_ref, send_ref):
    send_ref[...] = jnp.broadcast_to(reach_ref[...], send_ref.shape)


def reach_copies(devices, reach):
    per = reach.shape[0]
    return pl.pallas_call(
        copies_kernel,
        out_shape=jax.ShapeDtypeStruct((devices, per), jnp.float32),
        in_specs=[VMEM],
        out_specs=VMEM,
        name="reach_copies",
        **params(1, 10**10, 10**8),
    )(reach.reshape(1, per))


def level(width):
    return lax.broadcasted_iota(jnp.int32, (USED_RANKS, width), 0).astype(jnp.float32)


def slot_parts(slots):
    return [slice(low, min(low + 256, slots)) for low in range(0, slots, 256)]


def add_flops(first, last, rows_from, counts, rank_rows, own_rows, clear, holds, signs, place, sent):
    slots, rows = clear.shape
    runouts = holds.shape[0] // RANKS
    for low in range(0, runouts * RANKS, RANKS):
        holds[low + USED_RANKS : low + RANKS, :] = jnp.zeros((RANKS - USED_RANKS, slots), EXACT)
        signs[low + USED_RANKS : low + RANKS, :] = jnp.zeros((RANKS - USED_RANKS, rows), EXACT)

    parts = slot_parts(slots)
    tile = 32

    def hold(rank, low, part):
        shape = (tile, part.stop - part.start)
        rank = jnp.broadcast_to(rank[:, part].astype(jnp.int32), shape)
        rank = rank.astype(jnp.int8)
        down = lax.broadcasted_iota(jnp.int32, shape, 0)
        one, zero = jnp.ones(shape, EXACT), jnp.zeros(shape, EXACT)
        for step in range(0, USED_RANKS, tile):
            held = jnp.where(rank == (down + step).astype(jnp.int8), one, zero)
            holds[pl.ds(low + step, tile), part] = held

    def sign(at, low):
        rank = own_rows[pl.ds(at, 1), :]
        live = jnp.where(rank < NO_RANK, 1.0, 0.0)
        against = jnp.minimum(jnp.maximum(rank - level(rows), -1.0), 1.0)
        signs[pl.ds(low, USED_RANKS), :] = (against * live).astype(EXACT)

    def multiply(flop, depth, part):
        product = lax.dot_general(
            holds[:depth, part], signs[:depth, :], TN, preferred_element_type=jnp.float32
        )
        target, index = place(flop, part)
        target[index] = product.astype(jnp.bfloat16) * clear[part, :]

    def one_flop(flop, carry):
        count = counts[flop]
        row = (flop - rows_from) * runouts

        for few in range(1, runouts + 1):

            @pl.when(count == few)
            def _():
                for runout in range(few):
                    sign(row + runout, runout * RANKS)
                ranks = [rank_rows[pl.ds(row + runout, 1), :] for runout in range(few)]
                for chunk, part in enumerate(parts):
                    for runout, rank in enumerate(ranks):
                        hold(rank, runout * RANKS, part)
                    multiply(flop, few * RANKS, part)
                    sent(flop, chunk, part)

        return carry

    lax.fori_loop(first, last, one_flop, 0)


def first_kernel(
    count_ref, ranks_ref, boards_ref, cards_ref, pot_ref, act_ref,
    far_ref, near_ref, late_ranks, late_own, clear, weights_ref,
    counts, holds, signs, rank_rows, own_rows, sums, sem,
):
    read_counts(count_ref, counts)
    slots, rows = clear.shape
    total = ranks_ref.shape[0]
    places, flops, runouts = boards_ref.shape
    start = lax.axis_index("hand") * rows
    turn = lax.rem(slots - start, slots)

    cards = cards_ref[...]
    own_cards = pltpu.roll(cards, turn, 1)[:, :rows]
    card = lax.broadcasted_iota(jnp.int32, (CARDS, slots), 0)
    holders = jnp.where((card == cards[0:1]) | (card == cards[1:2]), 1.0, 0.0).astype(EXACT)
    card = lax.broadcasted_iota(jnp.int32, (CARDS, rows), 0)
    own_holders = (card == own_cards[0:1]) | (card == own_cards[1:2])
    own_holders = jnp.where(own_holders, 1.0, 0.0).astype(EXACT)

    boards = jnp.concatenate([boards_ref[place] for place in range(places)], axis=1)
    row = lax.broadcasted_iota(jnp.int32, (total, flops), 0)
    of_flop = row // runouts == lax.broadcasted_iota(jnp.int32, (total, flops), 1)
    spread = jnp.dot(
        jnp.where(of_flop, 1.0, 0.0).astype(jnp.bfloat16),
        boards.astype(jnp.float32).astype(jnp.bfloat16),
        preferred_element_type=jnp.float32,
    )
    row = lax.broadcasted_iota(jnp.int32, spread.shape, 0)
    lane = lax.broadcasted_iota(jnp.int32, spread.shape, 1)
    mine = lax.rem(row, runouts) == lax.rem(lane, runouts)
    card = lax.broadcasted_iota(jnp.int32, (total, CARDS), 1)
    on_board = card == DEAD_CARD
    for place in range(places):
        here = mine & (lane // runouts == place)
        found = jnp.sum(jnp.where(here, spread, 0.0), axis=1, keepdims=True)
        on_board = on_board | (card.astype(jnp.float32) == found)
    on_board = jnp.where(on_board, 1.0, 0.0).astype(EXACT)

    hits = jnp.dot(on_board, holders, preferred_element_type=jnp.float32)
    ranks = jnp.where(hits > 0.0, NO_RANK, ranks_ref[...].astype(jnp.float32))
    rank_rows[...] = ranks
    own_ranks = pltpu.roll(ranks, turn, 1)[:, :rows]
    own_rows[...] = own_ranks
    late_ranks[...] = ranks[total - late_ranks.shape[0] :]
    late_own[...] = own_ranks[total - late_own.shape[0] :]

    shared = lax.dot_general(holders, own_holders, TN, preferred_element_type=jnp.float32)
    clear[...] = jnp.maximum(1.0 - shared, 0.0).astype(jnp.bfloat16)

    act = act_ref[...]
    row = lax.broadcasted_iota(jnp.int32, (8, act.shape[1]), 0)
    weights = jnp.where(row == act, jnp.broadcast_to(pot_ref[...], row.shape), 0.0)
    weights_ref[...] = jnp.concatenate(split_bf16(weights), axis=0).astype(jnp.bfloat16)

    def copy(flop, chunk, part):
        span = pl.ds(part.start, part.stop - part.start)
        return pltpu.make_async_copy(
            sums.at[flop, span], far_ref.at[flop, span], sem.at[flop, chunk]
        )

    last = sums.shape[0]
    tables = (counts, rank_rows, own_rows, clear, holds, signs)
    add_flops(
        0, last, 0, *tables,
        lambda flop, part: (sums, (flop, part)),
        lambda flop, chunk, part: copy(flop, chunk, part).start(),
    )
    add_flops(
        last, last + 1, 0, *tables, lambda flop, part: (near_ref, part), lambda *done: None
    )
    for flop in range(last):
        for chunk, part in enumerate(slot_parts(slots)):
            copy(flop, chunk, part).wait()


def read_counts(count_ref, counts):
    for flop in range(count_ref.shape[1]):
        counts[flop] = count_ref[0, flop]


def showdown_scratch(flops, runouts, slots, rows):
    return [
        pltpu.SMEM((flops,), jnp.int32),
        pltpu.VMEM((runouts * RANKS, slots), EXACT),
        pltpu.VMEM((runouts * RANKS, rows), EXACT),
    ]


def first_flops(part, counts, ranks, boards, cards, pot, line_act, rows):
    total, slots = ranks.shape
    flops, lines = counts.shape[1], pot.shape[1]
    late = total // flops * (flops - part)
    return pl.pallas_call(
        first_kernel,
        out_shape=[
            jax.ShapeDtypeStruct((FAR_FLOPS, slots, rows), jnp.bfloat16),
            jax.ShapeDtypeStruct((slots, rows), jnp.bfloat16),
            jax.ShapeDtypeStruct((late, slots), jnp.float32),
            jax.ShapeDtypeStruct((late, rows), jnp.float32),
            jax.ShapeDtypeStruct((slots, rows), jnp.bfloat16),
            jax.ShapeDtypeStruct((8 * SPLITS, lines), jnp.bfloat16),
        ],
        in_specs=[VMEM] * 6,
        out_specs=[ANY] + [VMEM] * 5,
        scratch_shapes=showdown_scratch(flops, total // flops, slots, rows)
        + [
            pltpu.VMEM((total, slots), jnp.float32),
            pltpu.VMEM((total, rows), jnp.float32),
            pltpu.VMEM((part - 1, slots, rows), jnp.bfloat16),
            pltpu.SemaphoreType.DMA((part - 1, len(slot_parts(slots)))),
        ],
        name="first_flops",
        **params(FAR, 2 * 10**9, 10**7),
    )(counts, ranks, boards, cards, pot, line_act)


def other_kernel(
    part, count_ref, rank_rows, own_rows, clear, grouped_ref, far_ref, sums_ref,
    counts, holds, signs, sem,
):
    read_counts(count_ref, counts)
    copies = [
        pltpu.make_async_copy(far_ref.at[flop], sums_ref.at[flop], sem.at[flop])
        for flop in range(part - 1)
    ]
    for copy in copies:
        copy.start()
    tables = (counts, rank_rows, own_rows, clear, holds, signs)
    add_flops(
        part, count_ref.shape[1], part, *tables,
        lambda flop, part: (sums_ref, (flop, part)),
        lambda *done: None,
    )
    for copy in copies:
        copy.wait()


def other_flops(part, counts, rank_rows, own_rows, clear, grouped, far):
    slots, rows = clear.shape
    flops = counts.shape[1]
    return pl.pallas_call(
        functools.partial(other_kernel, part),
        out_shape=jax.ShapeDtypeStruct((flops, slots, rows), jnp.bfloat16),
        in_specs=[VMEM] * 4 + [ANY] * 2,
        out_specs=VMEM,
        scratch_shapes=showdown_scratch(flops, rank_rows.shape[0] // (flops - part), slots, rows)
        + [pltpu.SemaphoreType.DMA((part - 1,))],
        name="other_flops",
        **params(FAR, 2 * 10**9, 10**7),
    )(counts, rank_rows, own_rows, clear, grouped, far)


def split_bf16(values):
    parts = []
    for _ in range(SPLITS):
        part = values.astype(jnp.bfloat16).astype(jnp.float32)
        parts.append(part)
        values = values - part
    return parts


def action_kernel(reach_ref, strategy_ref, weights_ref, out_ref):
    flops, rows, lines = strategy_ref.shape
    senders, per = reach_ref.shape
    own = rows // per
    reach = reach_ref[...]
    slot = lax.broadcasted_iota(jnp.int32, (senders, per), 0) * per + lax.broadcasted_iota(
        jnp.int32, (senders, per), 1
    )
    alive = jnp.where(slot < HANDS, reach, 0.0)
    total = jnp.sum(jnp.sum(alive, axis=1, keepdims=True), axis=0, keepdims=True)

    mine = reach_ref[pl.ds(pl.multiple_of(lax.axis_index("hand") * own, 8), own), :]
    mine = jnp.concatenate(split_bf16(mine), axis=0).astype(jnp.bfloat16)
    row = lax.broadcasted_iota(jnp.int32, (rows, own * SPLITS), 0)
    low = lax.rem(lax.broadcasted_iota(jnp.int32, (rows, own * SPLITS), 1), own) * per
    sender = jnp.where((row >= low) & (row < low + per), 1.0, 0.0).astype(jnp.bfloat16)
    wide = jnp.dot(sender, mine, preferred_element_type=jnp.float32)
    row = lax.broadcasted_iota(jnp.int32, (rows, per), 0)
    lane = lax.broadcasted_iota(jnp.int32, (rows, per), 1)
    own_reach = jnp.sum(jnp.where(lax.rem(row, per) == lane, wide, 0.0), axis=1, keepdims=True)
    scale = jnp.broadcast_to(own_reach / total, (rows, lines))

    weights = weights_ref[...]
    for flop in range(flops):
        line_reach = (strategy_ref[flop].astype(jnp.float32) * scale).astype(jnp.bfloat16)
        parts = lax.dot_general(weights, line_reach, NT, preferred_element_type=jnp.float32)
        sums = parts[0:8] + parts[8:16] + parts[16:24]
        out_ref[flop * ACTS : (flop + 1) * ACTS, :] = sums[0:ACTS]


def action_sums(reach, strategy, weights):
    flops, rows, lines = strategy.shape
    return pl.pallas_call(
        action_kernel,
        out_shape=jax.ShapeDtypeStruct((flops * ACTS, rows), jnp.float32),
        in_specs=[VMEM] * 3,
        out_specs=VMEM,
        name="action_sums",
        **params(4, 10**8),
    )(reach, strategy, weights)


def row_span(flop):
    low = flop * ACTS // 8 * 8
    return low, (flop * ACTS + ACTS + 7) // 8 * 8


def response_kernel(single, count_ref, weight_ref, sums_ref, near_ref, *refs):
    shards, out_ref, products = refs[:-2], refs[-2], refs[-1]
    flops, slots, rows = sums_ref.shape
    gathered = jnp.zeros((flops * ACTS, slots), jnp.float32)
    for step, shard in enumerate(shards):
        at = jnp.bitwise_xor(lax.axis_index("hand"), step) * rows
        empty = jnp.zeros((flops * ACTS, slots - rows), jnp.float32)
        gathered = gathered + pltpu.roll(jnp.concatenate([shard[...], empty], axis=1), at, 1)
    splits = split_bf16(gathered)
    for flop in range(flops):
        matrix = near_ref if flop == single else sums_ref.at[flop]
        low, high = row_span(flop)
        left = jnp.concatenate([part[low:high] for part in splits], axis=0)
        products[flop, : left.shape[0]] = jnp.dot(
            left.astype(jnp.bfloat16), matrix[...], preferred_element_type=jnp.float32
        )

    values = jnp.zeros((1, rows), jnp.float32)
    weights = weight_ref[...].astype(jnp.float32)
    counts = count_ref[...].astype(jnp.float32)
    for flop in range(flops):
        low, high = row_span(flop)
        size, at = high - low, flop * ACTS - low
        group = sum(products[flop, part * size : (part + 1) * size] for part in range(SPLITS))
        best = jnp.max(group[at : at + ACTS], axis=0, keepdims=True)
        values = values + best * weights[:, flop : flop + 1] / counts[:, flop : flop + 1]
    tail = jnp.sum(weights, axis=1, keepdims=True)
    tail = jnp.broadcast_to(tail, (1, out_ref.shape[1] - rows))
    out_ref[...] = jnp.broadcast_to(jnp.concatenate([values, tail], axis=1), out_ref.shape)


def best_response(single, counts, weights, sums, near, shards, copies):
    rows = sums.shape[2]
    width = -(-(rows + 1) // 128) * 128
    return pl.pallas_call(
        functools.partial(response_kernel, single),
        out_shape=jax.ShapeDtypeStruct((copies, width), jnp.float32),
        in_specs=[VMEM] * (4 + len(shards)),
        out_specs=VMEM,
        scratch_shapes=[pltpu.VMEM((sums.shape[0], 16 * SPLITS, rows), jnp.float32)],
        name="best_response",
        **params(12, 10**9, 10**7),
    )(counts, weights, sums, near, *shards)


def finish_kernel(*refs):
    parts, out_ref = refs[:-1], refs[-1]
    rows = out_ref.shape[0]
    whole = sum(part[0] for part in parts)
    weight = whole[rows : rows + 1]
    out_ref[...] = whole[:rows] / weight


def finish(parts, rows):
    return pl.pallas_call(
        finish_kernel,
        out_shape=jax.ShapeDtypeStruct((rows,), jnp.float32),
        in_specs=[VMEM] * len(parts),
        out_specs=VMEM,
        name="finish",
        **params(2),
    )(*parts)


def board_parts(partial, boards_n):
    def swapped(values, mask):
        return lax.ppermute(values, "board", [(at, at ^ mask) for at in range(boards_n)])

    values, bit = partial + swapped(partial, 1), 2
    while True:
        masks = [bit, 2 * bit, 3 * bit] if 2 * bit < boards_n else [bit]
        parts = [values] + [swapped(values, mask) for mask in masks]
        bit *= 4
        if bit >= boards_n:
            return parts
        values = sum(parts)


def body(boards_n, hands_n, reach_pre, strategy, ranks, boards, river_live, iso_weight, pot, line_act):
    lines, rows = strategy.shape[1:]
    flops, runouts, slots = ranks.shape
    part = PART
    counts = river_live.reshape(1, flops)

    send = reach_copies(boards_n * hands_n, reach_pre)
    reach = lax.all_to_all(send, ("board", "hand"), 0, 0, tiled=True)
    far, near, *tables, weights = first_flops(
        part,
        counts,
        ranks.reshape(flops * runouts, slots),
        jnp.transpose(boards, (2, 0, 1)),
        hand_cards(),
        pot.reshape(1, lines),
        line_act.reshape(1, lines),
        rows,
    )

    grouped = action_sums(reach, jnp.swapaxes(strategy, 1, 2), weights)
    shards = [grouped]
    for step in range(1, hands_n):
        swap = [(source, source ^ step) for source in range(hands_n)]
        shards.append(lax.ppermute(grouped, "hand", swap))
    sums = other_flops(part, counts, *tables, grouped, far)

    weights = iso_weight.reshape(1, flops)
    partial = best_response(part - 1, counts, weights, sums, near, shards, 1)
    return finish(board_parts(partial, boards_n), rows)


def solution(mesh):
    in_specs = (
        P(("board", "hand")),
        P("board", None, "hand"),
        P("board", None, None),
        P("board", None, None),
        P("board"),
        P("board"),
        P(),
        P(),
    )
    run = functools.partial(body, mesh.shape["board"], mesh.shape["hand"])
    return jax.shard_map(run, mesh=mesh, in_specs=in_specs, out_specs=P("hand"), check_vma=False)
```
